256 devices in a mesh: grp: 32 (over z_hi, x, core), mem: 8 (over z_lo, y).
Axes of the slice: x: 4, y: 4, z: 8 (z_hi: 4, z_lo: 2; z = z_hi * 2 + z_lo), core: 2. Of those that a mesh axis runs over, the one named last changes fastest.
Arguments:
- picture_vectors: bfloat16 [16384, 1152], P(('grp', 'mem')), may hold values from -1.0234375 to 1.0234375
- caption_vectors: bfloat16 [16384, 1152], P(('grp', 'mem')), may hold values from -1.0234375 to 1.0234375
- matching_caption_position: int32 [16384], P('grp'), may hold values from 0 to 16383, each once
- learned_warmth_exponent: float32 [1], replicated, may hold values from 0.5 to 1.5
- offset_term: float32 [1], replicated, may hold values from -6 to -2
Outputs:
- image_grad: float32 [16384, 1152], P(('grp', 'mem'))
- text_grad: float32 [16384, 1152], P(('grp', 'mem'))
- statistics: float32 [3], replicated
The draws below stay inside these ranges and needn't reach their ends.
Inputs may be any that keep to these rules, and one draw needn't show every extreme that they name: `matching_caption_position`: it is a permutation of the text rows: every text row is the positive of exactly one image row.
All inputs are finite; a program needn't handle non-finite values.
Results may differ from the reference program's by a relative error of at most 0.0011.
Values may be sent and summed in bfloat16 or wider, within the bound.
A program may use at most 64 MiB of HBM per device.

```python
import math
import jax
import jax.numpy as jnp
from jax import lax

D = 1152
MATCHED_COUNT = 16384


def steps_of(key, extent, pieces, smallest, largest):
    level = 1.0
    for axis_at, shards_of in pieces:
        heights = jax.random.uniform(jax.random.fold_in(jax.random.fold_in(key, 6), axis_at), (shards_of,), jnp.float32, smallest / len(pieces), largest / len(pieces))
        level = level * jnp.repeat(jnp.exp(heights), extent[axis_at] // shards_of).reshape((-1,) + (1,) * (len(extent) - 1 - axis_at))
    return level


def centred(key, dims, width, most, shards=(), kind=jnp.bfloat16):
    values = width * jax.random.normal(key, dims, jnp.float32)
    if shards:
        values = values * steps_of(key, dims, shards, -0.22, 0.18)
    return jnp.clip(values, -most, most).astype(kind)


def setup_inputs(seed: int = 0) -> dict:
    key_list = jax.random.split(jax.random.key(seed), 6)
    return {
        "picture_vectors": centred(key_list[0], (MATCHED_COUNT, D), (D ** -0.25), 1.0234375, ((0, 256),)),
        "caption_vectors": centred(key_list[1], (MATCHED_COUNT, D), (D ** -0.25), 1.0234375, ((0, 256),)),
        "matching_caption_position": jax.random.permutation(key_list[2], MATCHED_COUNT).astype(jnp.int32),
        "learned_warmth_exponent": jnp.clip(jax.random.uniform(key_list[3], (1,), jnp.float32, 0.5, 1.5), 0.5, 1.5),
        "offset_term": jnp.clip(jax.random.uniform(key_list[4], (1,), jnp.float32, -6.0, -2.0), -6.0, -2.0),
    }


def reference(picture_vectors, caption_vectors, matching_caption_position, learned_warmth_exponent, offset_term):
    warmth_factor = jnp.exp(learned_warmth_exponent[0])
    offset_value = offset_term[0]
    block_rows = math.gcd(MATCHED_COUNT, 512)
    block_count = MATCHED_COUNT // block_rows
    columns = jnp.arange(MATCHED_COUNT, dtype=jnp.int32)
    image_blocks = picture_vectors.reshape(block_count, block_rows, D)
    label_blocks = matching_caption_position.reshape(block_count, block_rows)

    def block_step(state_now, inputs):
        text_acc, stat_sums = state_now
        image_block, label_block = inputs
        affinity_matrix = jnp.dot(image_block, caption_vectors.T, preferred_element_type=jnp.float32)
        matched_affinity = warmth_factor * affinity_matrix + offset_value
        label_sign = jnp.where(label_block[:, None] == columns[None, :], 1.0, -1.0).astype(affinity_matrix.dtype)
        accumulated_objective = -jnp.sum(jax.nn.log_sigmoid(label_sign * matched_affinity))
        derivative_factor = -label_sign * jax.nn.sigmoid(-label_sign * matched_affinity)
        sufficient_quantities = jnp.stack([accumulated_objective, jnp.sum(derivative_factor * warmth_factor * affinity_matrix), jnp.sum(derivative_factor)])
        coef_half = derivative_factor.astype(jnp.bfloat16)
        image_part = jnp.dot(coef_half, caption_vectors, preferred_element_type=jnp.float32)
        text_acc = text_acc + lax.dot_general(coef_half, image_block, (((0,), (0,)), ((), ())), preferred_element_type=jnp.float32)
        return (text_acc, stat_sums + sufficient_quantities), image_part

    initial = (jnp.zeros((MATCHED_COUNT, D), jnp.float32), jnp.zeros((3,), jnp.float32))
    (text_acc, stat_sums), image_parts = lax.scan(block_step, initial, (image_blocks, label_blocks))
    stretch_factor = warmth_factor / MATCHED_COUNT
    image_grad = image_parts.reshape(MATCHED_COUNT, D) * stretch_factor
    text_grad = text_acc * stretch_factor
    statistics = stat_sums / float(MATCHED_COUNT * MATCHED_COUNT)
    return image_grad, text_grad, statistics
```

```python
import jax
import jax.numpy as jnp
from jax import lax
from jax.experimental import pallas as pl
from jax.experimental.pallas import tpu as pltpu
from jax.sharding import PartitionSpec as P

MESH = pl.DeviceIdType.MESH
NX, NY, NZ = 4, 4, 8
ROWS = 64
HALF, QUARTER = 32, 16
D = 1152
TILE = 1024
PAIRS = 16384
LEVELS = 32000.0
BIAS = 256
BITS = 10

TEXT_ORDER = [(rx, ry) for rx in (2, 1, 3, 0) for ry in range(NY)]
IMAGE_ORDER = [
    (rc, rz) for part in ((4, 3, 5, 2), (6, 1, 7, 0)) for rc in (1, 0) for rz in part
]
TEXT_AT = {key: i * ROWS for i, key in enumerate(TEXT_ORDER)}
IMAGE_AT = {key: i * ROWS for i, key in enumerate(IMAGE_ORDER)}
N_COPIES = 256


def encode(values):
    top = jnp.max(jnp.abs(values), axis=1, keepdims=True)
    power = jnp.ceil(jnp.log2(jnp.maximum(top, 1e-36)))
    whole = jnp.round(values * (jnp.exp2(-power) * LEVELS)).astype(jnp.int32)
    lane = lax.broadcasted_iota(jnp.int32, (values.shape[0], 128), 1)
    code = power.astype(jnp.int32) + BIAS
    first = whole[:, :128]
    marked = (first & -2) | ((code >> jnp.minimum(lane, BITS)) & 1)
    first = jnp.where(lane < BITS, marked, first)
    return first.astype(jnp.int16), whole[:, 128:].astype(jnp.int16)


def decode(coded):
    whole = coded.astype(jnp.int32)
    lane = lax.broadcasted_iota(jnp.int32, (coded.shape[0], 128), 1)
    first = whole[:, :128]
    bits = jnp.where(lane < BITS, (first & 1) << jnp.minimum(lane, BITS), 0)
    code = jnp.sum(bits.astype(jnp.float32), axis=1, keepdims=True)
    return whole.astype(jnp.float32) * (jnp.exp2(code - BIAS) * (1.0 / LEVELS))


def fold(values):
    rows, columns = values.shape
    parts = [
        values[r : r + 8, c : c + 128]
        for r in range(0, rows, 8)
        for c in range(0, columns, 128)
    ]
    while len(parts) > 1:
        parts = [a + b for a, b in zip(parts[::2], parts[1::2], strict=True)]
    return parts[0]


def kernel(
    warmth_ref,
    offset_ref,
    labels_ref,
    image_hbm,
    text_hbm,
    image_out,
    text_out,
    stats_out,
    image,
    text,
    labels,
    label_row,
    scores,
    coef,
    image_sum,
    text_sum,
    coded_out,
    coded_in,
    stats,
    stat_slots,
    local_sem,
    send_sem,
    recv_sem,
):
    group, member = lax.axis_index("grp"), lax.axis_index("mem")
    core, x, z_high = lax.rem(group, 2), lax.rem(group // 2, NX), group // (2 * NX)
    y, z_low = lax.rem(member, NY), member // NY
    z = z_high * 2 + z_low

    def device(dx=0, dy=0, dz=0, dc=0):
        to_x, to_y = lax.rem(x + dx + NX, NX), lax.rem(y + dy + NY, NY)
        to_z, to_c = lax.rem(z + dz + NZ, NZ), lax.rem(core + dc, 2)
        return ((to_z // 2 * NX + to_x) * 2 + to_c, lax.rem(to_z, 2) * NY + to_y)

    right = {"x": device(dx=1), "y": device(dy=1), "z": device(dz=1)}
    left = {"x": device(dx=-1), "y": device(dy=-1), "z": device(dz=-1)}
    other = device(dc=1)

    image_at = {key: image.at[pl.ds(at, ROWS)] for key, at in IMAGE_AT.items()}
    own_image = pltpu.make_async_copy(image_hbm, image_at[0, 0], local_sem.at[0])
    own_text = pltpu.make_async_copy(
        text_hbm, text.at[pl.ds(TEXT_AT[0, 0], ROWS)], local_sem.at[1]
    )
    own_image.start()
    own_text.start()

    partners = [other]
    partners += [device(dx=d) for d in range(1, NX)]
    partners += [device(dy=d) for d in range(1, NY)]
    partners += [device(dz=d) for d in range(1, NZ)]
    barrier = pltpu.get_barrier_semaphore()
    for partner in partners:
        pl.semaphore_signal(barrier, inc=1, device_id=partner, device_id_type=MESH)
    pl.semaphore_wait(barrier, len(partners))

    copies = []

    def send(source, target, to):
        copy = pltpu.make_async_remote_copy(
            src_ref=source,
            dst_ref=target,
            send_sem=send_sem.at[len(copies)],
            recv_sem=recv_sem.at[len(copies)],
            device_id=to,
            device_id_type=MESH,
        )
        copies.append(copy)
        copy.start()
        return copy

    arrivals = {}

    def text_rows(key, row, rows):
        return text.at[pl.ds(TEXT_AT[key] + row, rows)]

    def send_text(key, row, rows, axis, step):
        rx, ry = key
        there = (
            ((rx - step) % NX, ry) if axis == "x" else (rx, (ry - step) % NY)
        )
        to = right[axis] if step == 1 else left[axis]
        arrivals[there, row] = send(
            text_rows(key, row, rows), text_rows(there, row, rows), to
        )

    def spread(key, row, rows, axis):
        send_text(key, row, rows, axis, 1)
        send_text(key, row, rows, axis, -1)

    def await_text(key, row):
        arrivals[key, row].wait_recv()

    def pass_on(key, row, axis):
        await_text(key, row)
        rel = key[0] if axis == "x" else key[1]
        if rel == 3:
            send_text(key, row, QUARTER, axis, 1)
        else:
            send_text(key, row + QUARTER, QUARTER, axis, -1)

    def send_image(key, row, rows, to, there):
        arrivals["image", there, row] = send(
            image.at[pl.ds(IMAGE_AT[key] + row, rows)],
            image.at[pl.ds(IMAGE_AT[there] + row, rows)],
            to,
        )

    own_text.wait()
    for row, axis in ((0, "x"), (HALF, "y")):
        spread((0, 0), row, HALF, axis)
    own_image.wait()
    send_image((0, 0), 0, ROWS, right["z"], (0, 7))
    send_image((0, 0), 0, ROWS, left["z"], (0, 1))
    for row, axis in ((0, "y"), (HALF, "x")):
        spread((0, 0), row, HALF, axis)
    send_image((0, 0), 0, ROWS, other, (1, 0))

    lane = lax.broadcasted_iota(jnp.int32, (8, 128), 1)
    mine = jnp.broadcast_to(labels_ref[pl.ds(member // 2, 1), :], (8, 128))
    turned = pltpu.roll(mine, 64, 1)
    in_upper = jnp.broadcast_to(lax.rem(member, 2), (8, 128)) == 1
    labels[0, 0] = jnp.where((lane >= 64) == in_upper, mine, turned)
    label_copies = []
    for d in range(1, NZ):
        label_copies.append(send(labels.at[0, 0], labels.at[0, NZ - d], device(dz=d)))

    def image_hop(rz):
        arrivals["image", (0, rz), 0].wait_recv()
        if rz in (7, 6):
            send_image((0, rz), 0, ROWS, right["z"], (0, rz - 1))
        elif rz == 5:
            send_image((0, rz), 0, HALF, right["z"], (0, 4))
        elif rz in (1, 2):
            send_image((0, rz), 0, ROWS, left["z"], (0, rz + 1))
        elif rz == 3:
            send_image((0, rz), HALF, HALF, left["z"], (0, 4))
        if rz == 4:
            arrivals["image", (0, 4), HALF].wait_recv()
        send_image((0, rz), 0, ROWS, other, (1, rz))

    for rel in (3, 1):
        pass_on((rel, 0), 0, "x")
        pass_on((0, rel), HALF, "y")
        spread((rel, 0), 0, HALF, "y")
        spread((0, rel), HALF, HALF, "x")
    image_hop(7)
    image_hop(1)
    for rel in (3, 1):
        pass_on((0, rel), 0, "y")
        pass_on((rel, 0), HALF, "x")
    for row in (0, QUARTER):
        await_text((2, 0), row)
        spread((2, 0), row, QUARTER, "y")
        await_text((0, 2), HALF + row)
        spread((0, 2), HALF + row, QUARTER, "x")
    image_hop(6)
    image_hop(2)
    for first in (3, 1):
        for rel in (3, 1):
            pass_on((first, rel), 0, "y")
            pass_on((rel, first), HALF, "x")
    image_hop(5)
    image_hop(3)
    for copy in label_copies:
        copy.wait_recv()
    label_other = send(labels.at[0], labels.at[1], other)
    for rel, row in ((3, 0), (1, QUARTER)):
        await_text((2, rel), row)
        send_text((2, rel), row, QUARTER, "y", 1 if rel == 3 else -1)
        await_text((rel, 2), HALF + row)
        send_text((rel, 2), HALF + row, QUARTER, "x", 1 if rel == 3 else -1)
    image_hop(4)
    await_text((2, 3), QUARTER)
    await_text((2, 1), 0)
    await_text((3, 2), HALF + QUARTER)
    await_text((1, 2), HALF)
    for rel in range(NX):
        await_text((rel, 2), 0)
        await_text((rel, 2), QUARTER)
        await_text((2, rel), HALF)
        await_text((2, rel), HALF + QUARTER)
    for rz in range(NZ):
        arrivals["image", (1, rz), 0].wait_recv()
    label_other.wait_recv()

    for at in range(0, TILE // ROWS, 2):
        (ca, za), (cb, zb) = IMAGE_ORDER[at], IMAGE_ORDER[at + 1]
        label_row[:, at * ROWS : (at + 2) * ROWS] = jnp.where(
            lane < 64, labels[ca, za], labels[cb, zb]
        )

    warmth = jnp.exp(jnp.full((1, 1), warmth_ref[0], jnp.float32))
    offset = offset_ref[0]
    zero = jnp.zeros((8, 128), jnp.float32)
    for i in range(3):
        stats[i] = zero

    def pairs(chunk):
        first = chunk * 256
        slot = chunk % 2
        scores[slot] = lax.dot_general(
            text[pl.ds(first, 256), :],
            image[...],
            (((1,), (1,)), ((), ())),
            preferred_element_type=jnp.float32,
        )
        for row in range(0, 256, 32):
            rx, ry = TEXT_ORDER[(first + row) // ROWS]
            owner_x, owner_y = lax.rem(x + rx, NX), lax.rem(y + ry, NY)
            base = (
                ((z_high * NX + owner_x) * 2 + core) * 8 + z_low * NY + owner_y
            ) * ROWS + row % ROWS
            position = lax.broadcasted_iota(jnp.int32, (32, 1), 0) + base
            for column in range(0, TILE, 256):
                at = pl.ds(column, 256)
                s = scores[slot, pl.ds(row, 32), at]
                logit = s * warmth + offset
                matched = label_row[0:1, at] == position
                signed = jnp.where(matched, -logit, logit)
                e = jnp.exp(-jnp.abs(signed))
                one_e = 1.0 + e
                inverse = 1.0 / one_e
                chance = jnp.where(signed >= 0, inverse, e * inverse)
                factor = jnp.where(matched, -chance, chance)
                coef[pl.ds(first + row, 32), at] = factor.astype(jnp.bfloat16)
                grown = zero
                for r in range(0, 32, 8):
                    for c in range(0, 256, 128):
                        part = slice(r, r + 8), slice(c, c + 128)
                        grown = grown * one_e[part] + e[part]
                stats[0] += fold(jnp.maximum(signed, 0.0)) + jnp.log1p(grown)
                stats[1] += fold(factor * s)
                stats[2] += fold(factor)

    def text_part(chunk):
        at = pl.ds(chunk * 256, 256)
        text_sum[at, :] = jnp.dot(
            coef[at, :], image[...], preferred_element_type=jnp.float32
        )

    def image_part(chunk):
        at = pl.ds(chunk * 256, 256)
        image_sum[at, :] = lax.dot_general(
            coef[:, at],
            text[...],
            (((0,), (0,)), ((), ())),
            preferred_element_type=jnp.float32,
        )

    place = [0]

    def send_sum(source, at, rows, to):
        start = place[0]
        place[0] += rows
        for r in range(0, rows, QUARTER):
            low, high = encode(source[pl.ds(at + r, QUARTER), :])
            coded_out[pl.ds(start + r, QUARTER), :128] = low
            coded_out[pl.ds(start + r, QUARTER), 128:] = high
        copy = send(
            coded_out.at[pl.ds(start, rows)], coded_in.at[pl.ds(start, rows)], to
        )
        return copy, start, rows

    def add_sum(sent, target, at):
        copy, start, rows = sent
        copy.wait_recv()
        for r in range(0, rows, QUARTER):
            target[pl.ds(at + r, QUARTER), :] += decode(
                coded_in[pl.ds(start + r, QUARTER), :]
            )

    def text_ring(axis, row, line):
        far, ahead, behind, here = (TEXT_AT[line[i]] + row for i in (2, 1, 3, 0))
        sent = {}

        def one():
            sent[1] = send_sum(text_sum, far, QUARTER, right[axis])
            sent[2] = send_sum(text_sum, far + QUARTER, QUARTER, left[axis])

        def two():
            add_sum(sent[1], text_sum, ahead)
            sent[3] = send_sum(text_sum, ahead, HALF, right[axis])
            add_sum(sent[2], text_sum, behind + QUARTER)
            sent[4] = send_sum(text_sum, behind, HALF, left[axis])

        def three():
            add_sum(sent[3], text_sum, here)
            add_sum(sent[4], text_sum, here)

        return one, two, three

    along_y = {rx: text_ring("y", 0, [(rx, i) for i in range(NY)]) for rx in range(NX)}
    along_x = {
        ry: text_ring("x", HALF, [(i, ry) for i in range(NX)]) for ry in range(NY)
    }
    last_x = text_ring("x", 0, [(i, 0) for i in range(NX)])
    last_y = text_ring("y", HALF, [(0, i) for i in range(NY)])

    for chunk in range(4):
        pairs(chunk)
    text_part(0)
    along_y[2][0]()
    for ry in (2, 1, 3, 0):
        along_x[ry][0]()
    text_part(1)
    along_y[1][0]()
    along_y[2][1]()
    text_part(2)
    along_y[3][0]()
    for ry in (2, 1, 3, 0):
        along_x[ry][1]()
    text_part(3)
    along_y[0][0]()
    along_y[1][1]()
    along_y[3][1]()
    along_y[2][2]()
    along_y[0][1]()

    sent_other = {}
    sent_z = {}

    def to_other(part):
        for rz in part:
            sent_other[rz] = send_sum(image_sum, IMAGE_AT[1, rz], ROWS, other)

    def from_other(part):
        for rz in part:
            add_sum(sent_other[rz], image_sum, IMAGE_AT[0, rz])

    def z_send(rz, row, to):
        sent_z[rz, row] = send_sum(image_sum, IMAGE_AT[0, rz] + row, HALF, to)

    def z_add(rz, row, target):
        add_sum(sent_z[rz, row], image_sum, IMAGE_AT[0, target] + row)

    image_part(0)
    to_other((4, 3, 5, 2))
    image_part(1)
    from_other((4, 3, 5, 2))
    z_send(4, 0, right["z"])
    z_send(4, HALF, left["z"])
    z_send(3, HALF, right["z"])
    z_send(5, 0, left["z"])
    image_part(2)
    to_other((6, 1, 7, 0))
    z_add(4, 0, 3)
    z_send(3, 0, right["z"])
    z_add(4, HALF, 5)
    z_send(5, HALF, left["z"])
    along_x[2][2]()
    last_y[0]()
    along_y[1][2]()
    along_y[3][2]()
    last_x[0]()
    image_part(3)
    from_other((6, 1, 7, 0))
    z_add(3, HALF, 2)
    z_send(2, HALF, right["z"])
    z_add(5, 0, 6)
    z_send(6, 0, left["z"])
    z_add(3, 0, 2)
    z_send(2, 0, right["z"])
    z_add(5, HALF, 6)
    z_send(6, HALF, left["z"])
    along_x[1][2]()
    along_x[3][2]()
    last_y[1]()
    last_x[1]()
    z_add(2, HALF, 1)
    z_send(1, HALF, right["z"])
    z_add(6, 0, 7)
    z_send(7, 0, left["z"])
    z_add(2, 0, 1)
    z_send(1, 0, right["z"])
    z_add(6, HALF, 7)
    z_send(7, HALF, left["z"])

    def total(slot):
        return jnp.concatenate(
            [jnp.sum(stats[i], axis=0, keepdims=True) for i in range(3)]
            + [jnp.zeros((5, 128), jnp.float32)],
            axis=0,
        ) if slot is None else slot

    running = total(None)
    base = 0
    for size, me, to in (
        (2, core, lambda d: device(dc=d)),
        (NX, x, lambda d: device(dx=d)),
        (NY, y, lambda d: device(dy=d)),
        (NZ, z, lambda d: device(dz=d)),
    ):
        stat_slots[base + me] = running
        sent = [
            send(stat_slots.at[base + me], stat_slots.at[base + me], to(d))
            for d in range(1, size)
        ]
        for copy in sent:
            copy.wait_recv()
        running = stat_slots[base]
        for i in range(1, size):
            running = running + stat_slots[base + i]
        base += size
    share = 1.0 / float(PAIRS * PAIRS)
    stats_out[0] = jnp.sum(running[0:1, :]) * share
    stats_out[1] = jnp.sum(running[1:2, :] * warmth) * share
    stats_out[2] = jnp.sum(running[2:3, :]) * share

    along_x[0][2]()
    along_y[0][2]()
    last_x[2]()
    last_y[2]()
    stretch = warmth * (1.0 / PAIRS)
    text_out[...] = text_sum[pl.ds(TEXT_AT[0, 0], ROWS), :] * stretch
    for row in (HALF, 0):
        z_add(1, row, 0)
    for row in (0, HALF):
        z_add(7, row, 0)
    image_out[...] = image_sum[pl.ds(IMAGE_AT[0, 0], ROWS), :] * stretch
    for copy in copies:
        copy.wait_send()


def on_device(picture, caption, labels, warmth, offset):
    vmem = pl.BlockSpec(memory_space=pltpu.VMEM)
    smem = pl.BlockSpec(memory_space=pltpu.SMEM)
    hbm = pl.BlockSpec(memory_space=pl.ANY)
    grad = jax.ShapeDtypeStruct((ROWS, D), jnp.float32)
    return pl.pallas_call(
        kernel,
        out_shape=(grad, grad, jax.ShapeDtypeStruct((3,), jnp.float32)),
        in_specs=[smem, smem, vmem, hbm, hbm],
        out_specs=(vmem, vmem, smem),
        scratch_shapes=[
            pltpu.VMEM((TILE, D), jnp.bfloat16),
            pltpu.VMEM((TILE, D), jnp.bfloat16),
            pltpu.VMEM((2, NZ, 8, 128), jnp.int32),
            pltpu.VMEM((8, TILE), jnp.int32),
            pltpu.VMEM((2, 256, TILE), jnp.float32),
            pltpu.VMEM((TILE, TILE), jnp.bfloat16),
            pltpu.VMEM((TILE, D), jnp.float32),
            pltpu.VMEM((TILE, D), jnp.float32),
            pltpu.VMEM((2048, D), jnp.int16),
            pltpu.VMEM((2048, D), jnp.int16),
            pltpu.VMEM((3, 8, 128), jnp.float32),
            pltpu.VMEM((2 + NX + NY + NZ, 8, 128), jnp.float32),
            pltpu.SemaphoreType.DMA((2,)),
            pltpu.SemaphoreType.DMA((N_COPIES,)),
            pltpu.SemaphoreType.DMA((N_COPIES,)),
        ],
        compiler_params=pltpu.CompilerParams(
            collective_id=0, has_side_effects=True, vmem_limit_bytes=56 << 20
        ),
    )(warmth, offset, labels.reshape(4, 128), picture, caption)


def solution(mesh):
    rows = P(("grp", "mem"), None)
    return jax.shard_map(
        on_device,
        mesh=mesh,
        in_specs=(rows, rows, P("grp"), P(), P()),
        out_specs=(rows, rows, P()),
        check_vma=False,
    )
```

```python
import jax
import jax.numpy as jnp
from jax import lax
from jax.experimental import pallas as pl
from jax.experimental.pallas import tpu as pltpu
from jax.sharding import PartitionSpec as P

MESH = pl.DeviceIdType.MESH
NX, NY, NZ = 4, 4, 8
ROWS = 64
HALF, QUARTER = 32, 16
D = 1152
LANES = 128
WIDE = D // LANES
TILE = 1024
PAIRS = 16384
LEVELS = 32000.0
SMALLEST = 1e-30

FAR_FIRST = (2, 1, 3, 0)
TEXT_HALVES = [
    (h, i, j)
    for i in FAR_FIRST
    for h in (0, 1)
    for j in (FAR_FIRST if h == 0 else FAR_FIRST[::-1])
]
TEXT_AT = {key: n * HALF for n, key in enumerate(TEXT_HALVES)}
IMAGE_ORDER = [
    (c, d) for part in ((4, 3, 5, 2), (6, 1, 7, 0)) for c in (1, 0) for d in part
]
IMAGE_AT = {key: n * ROWS for n, key in enumerate(IMAGE_ORDER)}
N_SEND, N_RECV = 6, 91
N_TILES = 1142


def fold(values):
    rows, columns = values.shape
    parts = [
        values[r : r + 8, c : c + LANES]
        for r in range(0, rows, 8)
        for c in range(0, columns, LANES)
    ]
    while len(parts) > 1:
        parts = [a + b for a, b in zip(parts[::2], parts[1::2], strict=True)]
    return parts[0]


def kernel(
    warmth_ref,
    offset_ref,
    labels_ref,
    image_hbm,
    text_hbm,
    image_out,
    text_out,
    stats_out,
    image,
    text,
    labels,
    label_row,
    scores,
    coef,
    image_sum,
    text_sum,
    image_top,
    text_top,
    coded_out,
    coded_in,
    stats,
    stat_slots,
    local_sem,
    send_sem,
    recv_sem,
):
    group, member = lax.axis_index("grp"), lax.axis_index("mem")
    core, x, z_high = lax.rem(group, 2), lax.rem(group // 2, NX), group // (2 * NX)
    y, z_low = lax.rem(member, NY), member // NY
    z = z_high * 2 + z_low

    def device(dx=0, dy=0, dz=0, dc=0):
        to_x, to_y = lax.rem(x + dx + NX, NX), lax.rem(y + dy + NY, NY)
        to_z, to_c = lax.rem(z + dz + NZ, NZ), lax.rem(core + dc, 2)
        return ((to_z // 2 * NX + to_x) * 2 + to_c, lax.rem(to_z, 2) * NY + to_y)

    ahead = {"x": device(dx=1), "y": device(dy=1), "z": device(dz=1)}
    behind = {"x": device(dx=-1), "y": device(dy=-1), "z": device(dz=-1)}
    other = device(dc=1)

    own_image = pltpu.make_async_copy(
        image_hbm, image.at[pl.ds(IMAGE_AT[0, 0], ROWS)], local_sem.at[0]
    )
    own_text = pltpu.make_async_copy(
        text_hbm, text.at[pl.ds(TEXT_AT[0, 0, 0], ROWS)], local_sem.at[1]
    )
    own_image.start()
    own_text.start()

    partners = [other]
    partners += [device(dx=d) for d in range(1, NX)]
    partners += [device(dy=d) for d in range(1, NY)]
    partners += [device(dz=d) for d in range(1, NZ)]
    barrier = pltpu.get_barrier_semaphore()
    for partner in partners:
        pl.semaphore_signal(barrier, inc=1, device_id=partner, device_id_type=MESH)
    pl.semaphore_wait(barrier, len(partners))

    recv_of, sent_of = {}, {}

    def place(key):
        return recv_sem.at[recv_of.setdefault(key, len(recv_of))]

    def send(kind, amount, source, target, to, key):
        at = list(sent_of).index(kind) if kind in sent_of else len(sent_of)
        sent_of[kind] = sent_of.get(kind, 0) + amount
        pltpu.make_async_remote_copy(
            src_ref=source,
            dst_ref=target,
            send_sem=send_sem.at[at],
            recv_sem=place(key),
            device_id=to,
            device_id_type=MESH,
        ).start()

    def expect(key, ref):
        pltpu.make_async_remote_copy(
            src_ref=ref,
            dst_ref=ref,
            send_sem=send_sem.at[0],
            recv_sem=place(key),
            device_id=other,
            device_id_type=MESH,
        ).wait_recv()

    def all_sent(refs):
        for at, (kind, amount) in enumerate(sent_of.items()):
            ref = refs[kind].at[pl.ds(0, amount)]
            pltpu.make_async_remote_copy(
                src_ref=ref,
                dst_ref=ref,
                send_sem=send_sem.at[at],
                recv_sem=recv_sem.at[0],
                device_id=other,
                device_id_type=MESH,
            ).wait_send()

    def axis_of(h, nth):
        return "xy"[(h + nth) % 2]

    def text_key(h, i, j):
        return ("rest", h) if j == 2 else ("text", h, i, j)

    def send_text(h, i, j, row, rows, nth, step):
        there = (h, (i - step) % 4, j) if nth == 0 else (h, i, (j - step) % 4)
        send(
            "text",
            rows,
            text.at[pl.ds(TEXT_AT[h, i, j] + row, rows)],
            text.at[pl.ds(TEXT_AT[there] + row, rows)],
            (ahead if step == 1 else behind)[axis_of(h, nth)],
            text_key(*there),
        )

    def spread(h, i, j, nth):
        send_text(h, i, j, 0, HALF, nth, 1)
        send_text(h, i, j, 0, HALF, nth, -1)

    def await_text(h, i, j):
        expect(text_key(h, i, j), text.at[pl.ds(0, HALF)])

    def pass_on(h, i, j, nth):
        if (i, j)[nth] == 3:
            send_text(h, i, j, 0, QUARTER, nth, 1)
        else:
            send_text(h, i, j, QUARTER, QUARTER, nth, -1)

    def send_image(c, d, row, to, there):
        send(
            "image",
            HALF,
            image.at[pl.ds(IMAGE_AT[c, d] + row, HALF)],
            image.at[pl.ds(IMAGE_AT[there] + row, HALF)],
            to,
            "across" if there[0] else ("image", there[1], row),
        )

    def image_hop(d, row):
        expect(("image", d, row), image.at[pl.ds(0, HALF)])
        if d > 5 or (d == 5 and row == 0):
            send_image(0, d, row, ahead["z"], (0, d - 1))
        if d < 3 or (d == 3 and row == HALF):
            send_image(0, d, row, behind["z"], (0, d + 1))
        send_image(0, d, row, other, (1, d))

    own_text.wait()
    for h in (0, 1):
        spread(h, 0, 0, 0)
    own_image.wait()
    send_image(0, 0, 0, ahead["z"], (0, 7))
    send_image(0, 0, HALF, behind["z"], (0, 1))
    for h in (0, 1):
        spread(h, 0, 0, 1)
    send_image(0, 0, HALF, ahead["z"], (0, 7))
    send_image(0, 0, 0, behind["z"], (0, 1))
    for row in (0, HALF):
        send_image(0, 0, row, other, (1, 0))

    lane = lax.broadcasted_iota(jnp.int32, (8, LANES), 1)
    mine = jnp.broadcast_to(labels_ref[pl.ds(member // 2, 1), :], (8, LANES))
    turned = pltpu.roll(mine, ROWS, 1)
    in_upper = jnp.broadcast_to(lax.rem(member, 2), (8, LANES)) == 1
    labels[0, 0] = jnp.where((lane >= ROWS) == in_upper, mine, turned)
    for d in range(1, NZ):
        there = labels.at[0, NZ - d]
        send("label", 1, labels.at[0, 0], there, device(dz=d), "label")

    for i in (3, 1):
        for h in (0, 1):
            await_text(h, i, 0)
            pass_on(h, i, 0, 0)
            spread(h, i, 0, 1)
    image_hop(7, 0)
    image_hop(1, HALF)
    for j in (3, 1):
        for h in (0, 1):
            await_text(h, 0, j)
            pass_on(h, 0, j, 1)
    image_hop(7, HALF)
    image_hop(1, 0)
    for h in (0, 1):
        await_text(h, 2, 0)
        spread(h, 2, 0, 1)
    image_hop(6, 0)
    image_hop(2, HALF)
    for i in (3, 1):
        for j in (3, 1):
            for h in (0, 1):
                await_text(h, i, j)
                pass_on(h, i, j, 1)
        image_hop((6, 5)[i == 1], (HALF, 0)[i == 1])
        image_hop((2, 3)[i == 1], (0, HALF)[i == 1])
    expect("label", labels.at[0, pl.ds(1, NZ - 1)])
    send("labels", 1, labels.at[pl.ds(0, 1)], labels.at[pl.ds(1, 1)], other, "labels")
    image_hop(5, HALF)
    image_hop(3, 0)
    for j in (3, 1):
        for h in (0, 1):
            await_text(h, 2, j)
            pass_on(h, 2, j, 1)
    image_hop(4, 0)
    image_hop(4, HALF)
    for h in (0, 1):
        expect(("rest", h), text.at[pl.ds(0, 4 * HALF)])
    expect("labels", labels.at[pl.ds(0, 1)])
    expect("across", image.at[pl.ds(0, NZ * ROWS)])

    for at in range(0, TILE // ROWS, 2):
        label_row[:, at * ROWS : (at + 2) * ROWS] = jnp.where(
            lane < ROWS, labels[IMAGE_ORDER[at]], labels[IMAGE_ORDER[at + 1]]
        )

    warmth = jnp.exp(jnp.full((1, 1), warmth_ref[0], jnp.float32))
    offset = offset_ref[0]
    zero = jnp.zeros((8, LANES), jnp.float32)
    for n in range(3):
        stats[n] = zero

    def pairs(chunk):
        first = chunk * 256
        slot = chunk % 2
        scores[slot] = lax.dot_general(
            text[pl.ds(first, 256), :],
            image[...],
            (((1,), (1,)), ((), ())),
            preferred_element_type=jnp.float32,
        )
        for row in range(0, 256, HALF):
            h, i, j = TEXT_HALVES[(first + row) // HALF]
            rx, ry = (i, j) if h == 0 else (j, i)
            owner_x, owner_y = lax.rem(x + rx, NX), lax.rem(y + ry, NY)
            base = (
                ((z_high * NX + owner_x) * 2 + core) * 8 + z_low * NY + owner_y
            ) * ROWS + h * HALF
            position = lax.broadcasted_iota(jnp.int32, (HALF, 1), 0) + base
            for column in range(0, TILE, 256):
                at = pl.ds(column, 256)
                s = scores[slot, pl.ds(row, HALF), at]
                logit = s * warmth + offset
                matched = label_row[0:1, at] == position
                signed = jnp.where(matched, -logit, logit)
                e = jnp.exp(-jnp.abs(signed))
                one_e = 1.0 + e
                inverse = 1.0 / one_e
                chance = jnp.where(signed >= 0, inverse, e * inverse)
                factor = jnp.where(matched, -chance, chance)
                coef[pl.ds(first + row, HALF), at] = factor.astype(jnp.bfloat16)
                grown = zero
                for r in range(0, HALF, 8):
                    for c in range(0, 256, LANES):
                        part = slice(r, r + 8), slice(c, c + LANES)
                        grown = grown * one_e[part] + e[part]
                stats[0] += fold(jnp.maximum(signed, 0.0)) + jnp.log1p(grown)
                stats[1] += fold(factor * s)
                stats[2] += fold(factor)

    def find_tops(sums, tops, first):
        for row in range(first, first + 256, HALF):
            top = None
            for r in range(0, HALF, 8):
                for c in range(0, D, LANES):
                    part = jnp.abs(sums[pl.ds(row + r, 8), c : c + LANES])
                    top = part if top is None else jnp.maximum(top, part)
            top = jnp.max(jnp.max(top, axis=1, keepdims=True), axis=0, keepdims=True)
            tops[row // HALF] = jnp.broadcast_to(top, (QUARTER, LANES))

    def text_part(chunk):
        at = pl.ds(chunk * 256, 256)
        text_sum[at, :] = jnp.dot(
            coef[at, :], image[...], preferred_element_type=jnp.float32
        )
        find_tops(text_sum, text_top, chunk * 256)

    def image_part(chunk):
        at = pl.ds(chunk * 256, 256)
        image_sum[at, :] = lax.dot_general(
            coef[:, at],
            text[...],
            (((0,), (0,)), ((), ())),
            preferred_element_type=jnp.float32,
        )
        find_tops(image_sum, image_top, chunk * 256)

    messages = {}
    used = [0]

    def arrived(parts):
        found = {}
        for adds in parts:
            for name, _ in adds:
                power = coded_in[messages[name]].astype(jnp.float32)
                bound = jnp.exp2(power)
                found[name] = bound * (1.0 / LEVELS), bound
        return found

    def summed(sums, row, wide, adds, found):
        value = sums[pl.ds(row, QUARTER), wide * LANES : (wide + 1) * LANES]
        for name, nth in adds:
            tile = coded_in[messages[name] + 1 + nth * WIDE + wide]
            value = value + tile.astype(jnp.float32) * found[name][0]
        return value

    def send_sum(name, sums, tops, row, parts, to, key):
        start, count = used[0], 1 + len(parts) * WIDE
        messages[name] = start
        used[0] += count
        found = arrived(parts)
        bound = tops[row // HALF]
        if len(parts) * QUARTER > HALF:
            bound = jnp.maximum(bound, tops[row // HALF + 1])
        for _, more in found.values():
            bound = bound + more
        power = jnp.ceil(jnp.log2(jnp.maximum(bound, SMALLEST)))
        coded_out[start] = power.astype(jnp.int16)
        scale = jnp.exp2(-power) * LEVELS
        for n, adds in enumerate(parts):
            for wide in range(WIDE):
                value = summed(sums, row + n * QUARTER, wide, adds, found)
                coded_out[start + 1 + n * WIDE + wide] = (
                    jnp.round(value * scale).astype(jnp.int32).astype(jnp.int16)
                )
        at = pl.ds(start, count)
        send("sum", count, coded_out.at[at], coded_in.at[at], to, key)

    def await_sum(key, *sizes):
        count = sum(1 + rows // QUARTER * WIDE for rows in sizes)
        expect(key, coded_in.at[pl.ds(0, count)])

    def text_send(name, at, row, parts, to):
        send_sum(name, text_sum, text_top, at + row, parts, to, name)

    def second_far(i):
        for h in (0, 1):
            axis, at = axis_of(h, 1), TEXT_AT[h, i, 2]
            text_send((h, i, "fa"), at, 0, [[]], ahead[axis])
            text_send((h, i, "fb"), at, QUARTER, [[]], behind[axis])

    def second_near(i):
        for h in (0, 1):
            axis = axis_of(h, 1)
            await_sum((h, i, "fa"), QUARTER)
            parts = [[((h, i, "fa"), 0)], []]
            name = (h, i, "na")
            send_sum(
                name, text_sum, text_top, TEXT_AT[h, i, 1], parts, ahead[axis], (h, i, "n")
            )
            await_sum((h, i, "fb"), QUARTER)
            parts = [[], [((h, i, "fb"), 0)]]
            name = (h, i, "nb")
            send_sum(
                name, text_sum, text_top, TEXT_AT[h, i, 3], parts, behind[axis], (h, i, "n")
            )

    def second_done(i):
        for h in (0, 1):
            await_sum((h, i, "n"), HALF, HALF)

    def line(h, i, nth):
        return [((h, i, "na"), nth), ((h, i, "nb"), nth)]

    def first_far():
        for h in (0, 1):
            axis, at = axis_of(h, 0), TEXT_AT[h, 2, 0]
            text_send((h, "fa"), at, 0, [line(h, 2, 0)], ahead[axis])
            text_send((h, "fb"), at, QUARTER, [line(h, 2, 1)], behind[axis])

    def first_near(i):
        for h in (0, 1):
            axis = axis_of(h, 0)
            far = "fa" if i == 1 else "fb"
            await_sum((h, far), QUARTER)
            parts = [line(h, i, 0), line(h, i, 1)]
            parts[i == 3].append(((h, far), 0))
            send_sum(
                (h, "n", i),
                text_sum,
                text_top,
                TEXT_AT[h, i, 0],
                parts,
                (ahead if i == 1 else behind)[axis],
                (h, "n"),
            )

    def text_last():
        for h in (0, 1):
            await_sum((h, "n"), HALF, HALF)
            for n in (0, 1):
                adds = line(h, 0, n) + [((h, "n", 1), n), ((h, "n", 3), n)]
                found = arrived([adds])
                at = h * HALF + n * QUARTER
                for wide in range(WIDE):
                    value = summed(
                        text_sum, TEXT_AT[h, 0, 0] + n * QUARTER, wide, adds, found
                    )
                    text_out[at : at + QUARTER, wide * LANES : (wide + 1) * LANES] = (
                        value * stretch
                    )

    def to_other(part):
        for d in part:
            send_sum(
                ("c", d), image_sum, image_top, IMAGE_AT[1, d], [[]] * 4, other, ("c", part)
            )

    def from_other(part):
        await_sum(("c", part), *[ROWS] * len(part))

    def z_adds(d, row, n):
        adds = [(("c", d), row // QUARTER + n)]
        if d < 4 and (d < 3 or row == 0):
            adds.append((("za", d + 1, row), n))
        if (d > 4 or d == 0) and (d != 5 or row == HALF):
            adds.append((("zb", (d - 1) % NZ, row), n))
        return adds

    def z_send(d, row, way, wait=True):
        came = [a[0] for a in z_adds(d, row, 0)[1:]]
        for name in came:
            await_sum(name, HALF)
        name = ("z" + way, d, row)
        parts = [z_adds(d, row, n) for n in (0, 1)]
        to = (ahead if way == "a" else behind)["z"]
        send_sum(name, image_sum, image_top, IMAGE_AT[0, d] + row, parts, to, name)

    def image_last():
        for row in (0, HALF):
            for name in (("za", 1, row), ("zb", 7, row)):
                await_sum(name, HALF)
            for n in (0, 1):
                adds = z_adds(0, row, n)
                found = arrived([adds])
                at = row + n * QUARTER
                for wide in range(WIDE):
                    value = summed(
                        image_sum, IMAGE_AT[0, 0] + at, wide, adds, found
                    )
                    image_out[at : at + QUARTER, wide * LANES : (wide + 1) * LANES] = (
                        value * stretch
                    )

    stat_axes = (
        (2, core, lambda d: device(dc=d)),
        (NX, x, lambda d: device(dx=d)),
        (NY, y, lambda d: device(dy=d)),
        (NZ, z, lambda d: device(dz=d)),
    )

    def stat_send(nth, value):
        base = sum(a[0] for a in stat_axes[:nth])
        size, me, to = stat_axes[nth]
        stat_slots[base + me] = value
        for d in range(1, size):
            slot = stat_slots.at[pl.ds(base + me, 1)]
            send("stat", 1, slot, slot, to(d), ("stat", nth))

    def stat_sum(nth):
        base, size = sum(a[0] for a in stat_axes[:nth]), stat_axes[nth][0]
        expect(("stat", nth), stat_slots.at[pl.ds(0, size - 1)])
        value = stat_slots[base]
        for n in range(1, size):
            value = value + stat_slots[base + n]
        return value

    stretch = warmth * (1.0 / PAIRS)
    near_part, far_part = (6, 1, 7, 0), (4, 3, 5, 2)

    for chunk in range(4):
        pairs(chunk)
    stat_send(
        0,
        jnp.concatenate(
            [jnp.sum(stats[n], axis=0, keepdims=True) for n in range(3)]
            + [jnp.zeros((5, LANES), jnp.float32)],
            axis=0,
        ),
    )
    image_part(0)
    to_other(far_part)
    text_part(0)
    second_far(2)
    image_part(1)
    stat_send(1, stat_sum(0))
    from_other(far_part)
    z_send(4, 0, "a")
    z_send(4, HALF, "b")
    z_send(3, HALF, "a")
    z_send(5, 0, "b")
    text_part(1)
    second_far(1)
    second_near(2)
    image_part(2)
    to_other(near_part)
    stat_send(2, stat_sum(1))
    z_send(3, 0, "a")
    z_send(5, HALF, "b")
    text_part(2)
    second_far(3)
    second_near(1)
    second_done(2)
    first_far()
    z_send(2, HALF, "a")
    text_part(3)
    second_far(0)
    second_near(3)
    image_part(3)
    from_other(near_part)
    z_send(6, 0, "b")
    z_send(2, 0, "a")
    z_send(6, HALF, "b")
    second_done(1)
    first_near(1)
    second_near(0)
    z_send(1, HALF, "a")
    z_send(7, 0, "b")
    second_done(3)
    first_near(3)
    stat_send(3, stat_sum(2))
    z_send(1, 0, "a")
    z_send(7, HALF, "b")
    second_done(0)
    text_last()
    everyone = stat_sum(3)
    share = 1.0 / float(PAIRS * PAIRS)
    stats_out[0] = jnp.sum(everyone[0:1, :]) * share
    stats_out[1] = jnp.sum(everyone[1:2, :] * warmth) * share
    stats_out[2] = jnp.sum(everyone[2:3, :]) * share
    image_last()
    all_sent(
        {
            "text": text,
            "image": image,
            "label": labels.at[0],
            "labels": labels,
            "sum": coded_out,
            "stat": stat_slots,
        }
    )


def on_device(picture, caption, labels, warmth, offset):
    vmem = pl.BlockSpec(memory_space=pltpu.VMEM)
    smem = pl.BlockSpec(memory_space=pltpu.SMEM)
    hbm = pl.BlockSpec(memory_space=pl.ANY)
    grad = jax.ShapeDtypeStruct((ROWS, D), jnp.float32)
    return pl.pallas_call(
        kernel,
        out_shape=(grad, grad, jax.ShapeDtypeStruct((3,), jnp.float32)),
        in_specs=[smem, smem, vmem, hbm, hbm],
        out_specs=(vmem, vmem, smem),
        scratch_shapes=[
            pltpu.VMEM((TILE, D), jnp.bfloat16),
            pltpu.VMEM((TILE, D), jnp.bfloat16),
            pltpu.VMEM((2, NZ, 8, LANES), jnp.int32),
            pltpu.VMEM((8, TILE), jnp.int32),
            pltpu.VMEM((2, 256, TILE), jnp.float32),
            pltpu.VMEM((TILE, TILE), jnp.bfloat16),
            pltpu.VMEM((TILE, D), jnp.float32),
            pltpu.VMEM((TILE, D), jnp.float32),
            pltpu.VMEM((TILE // HALF, QUARTER, LANES), jnp.float32),
            pltpu.VMEM((TILE // HALF, QUARTER, LANES), jnp.float32),
            pltpu.VMEM((N_TILES, QUARTER, LANES), jnp.int16),
            pltpu.VMEM((N_TILES, QUARTER, LANES), jnp.int16),
            pltpu.VMEM((3, 8, LANES), jnp.float32),
            pltpu.VMEM((2 + NX + NY + NZ, 8, LANES), jnp.float32),
            pltpu.SemaphoreType.DMA((2,)),
            pltpu.SemaphoreType.DMA((N_SEND,)),
            pltpu.SemaphoreType.DMA((N_RECV,)),
        ],
        compiler_params=pltpu.CompilerParams(
            collective_id=0, has_side_effects=True, vmem_limit_bytes=56 << 20
        ),
    )(warmth, offset, labels.reshape(4, LANES), picture, caption)


def solution(mesh):
    rows = P(("grp", "mem"), None)
    return jax.shard_map(
        on_device,
        mesh=mesh,
        in_specs=(rows, rows, P("grp"), P(), P()),
        out_specs=(rows, rows, P()),
        check_vma=False,
    )
```

```python
import jax
import jax.numpy as jnp
from jax import lax
from jax.experimental import pallas as pl
from jax.experimental.pallas import tpu as pltpu
from jax.sharding import PartitionSpec as P

MESH = pl.DeviceIdType.MESH
NX, NY, NZ = 4, 4, 8
ROWS = 64
HALF, QUARTER = 32, 16
D = 1152
LANES = 128
WIDE = D // LANES
TILE = 1024
PAIRS = 16384
LEVELS = 32000.0
SMALLEST = 1e-30

FAR_FIRST = (2, 1, 3, 0)
TEXT_HALVES = [
    (h, i, j)
    for i in FAR_FIRST
    for h in (0, 1)
    for j in (FAR_FIRST if h == 0 else FAR_FIRST[::-1])
]
TEXT_AT = {key: n * HALF for n, key in enumerate(TEXT_HALVES)}
PARTS = ((4, 3), (5, 2), (6, 1), (7, 0))
IMAGE_ORDER = [(c, d) for part in PARTS for c in (1, 0) for d in part]
IMAGE_AT = {key: n * ROWS for n, key in enumerate(IMAGE_ORDER)}
N_SEND, N_RECV = 6, 126
N_TILES = 1152
ORDER = [
    "begin", ("z", 7, 0), ("z", 1, 48), ("t", 0, 3, 0), ("t", 0, 1, 0), ("t", 1, 3, 0), ("t", 1, 1, 0),
    ("z", 1, 32), ("z", 7, 16), ("z", 7, 32), ("z", 1, 16), ("z", 7, 48), ("z", 1, 0), ("t", 0, 2, 0),
    ("t", 1, 2, 0), ("t", 1, 0, 3), ("t", 1, 0, 1), "label", ("c", 3), ("z", 2, 48), ("z", 6, 0),
    ("t", 0, 0, 3), ("t", 0, 0, 1), ("z", 2, 32), ("z", 6, 16), "labels", ("t", 1, 3, 3), ("t", 0, 3, 3),
    ("t", 0, 3, 1), ("z", 2, 16), ("t", 1, 3, 1), ("z", 6, 32), ("z", 2, 0), ("z", 6, 48), ("t", 1, 1, 3),
    ("t", 1, 1, 1), ("t", 0, 1, 1), ("t", 0, 1, 3), ("z", 3, 48), ("z", 5, 0), ("c", 2), ("t", 1, 2, 3),
    ("t", 1, 2, 1), ("t", 0, 2, 3), ("t", 0, 2, 1), ("z", 3, 32), ("z", 5, 16), ("z", 3, 16), ("z", 5, 32),
    ("z", 3, 0), ("z", 5, 48), ("t", 1, 2, 2), ("t", 1, 0, 2), ("t", 0, 2, 2), ("p", 0, 1), ("t", 0, 0, 2),
    ("p", 3, 1), ("c", 1), ("t", 0, 3, 2), ("t", 1, 3, 2), ("p", 2, 1), ("t", 1, 1, 2), ("z", 4, 48),
    ("z", 4, 32), ("z", 4, 0), ("z", 4, 16), ("t", 0, 1, 2), ("p", 1, 1), ("I", 2), ("c", 0), ("p", 1, 0),
    ("p", 0, 0), ("p", 2, 0), ("p", 3, 0), ("s", 0), ("T", 1), ("sf", 1), ("I", 0), ("co", 0), ("T", 0),
    ("sf", 2), ("cw", 4), ("zs", 4, 16), ("zs", 4, 0), ("cw", 3), ("I", 1), ("s", 1), ("co", 1), ("T", 2),
    ("sf", 3), ("cw", 5), ("zs", 3, 32), ("zs", 3, 16), ("zs", 3, 48), ("sn", 2), ("zs", 3, 0), ("sn", 1),
    ("cw", 2), ("co", 2), ("T", 3), ("sf", 0), ("s", 2), ("cw", 6), ("zs", 2, 32), ("sn", 3), ("zs", 2, 16),
    ("I", 3), ("zs", 2, 48), ("zs", 2, 0), ("co", 3), ("cw", 1), ("sn", 0), ("f", 2), ("f", 1), ("cw", 7),
    ("zs", 1, 32), ("zs", 1, 16), ("cw", 0), ("s", 3), ("zs", 1, 48), ("f", 3), ("zs", 1, 0), ("zl", 16),
    ("zl", 32), ("zl", 0), ("zl", 48), ("tl", 1), ("tl", 0), ("s", 4),
]


def fold(values):
    rows, columns = values.shape
    parts = [
        values[r : r + 8, c : c + LANES]
        for r in range(0, rows, 8)
        for c in range(0, columns, LANES)
    ]
    while len(parts) > 1:
        parts = [a + b for a, b in zip(parts[::2], parts[1::2], strict=True)]
    return parts[0]


def kernel(
    warmth_hbm,
    offset_hbm,
    labels_ref,
    image_hbm,
    text_hbm,
    image_out,
    text_out,
    stats_out,
    image,
    text,
    labels,
    label_row,
    scores,
    coef,
    image_sum,
    text_sum,
    image_top,
    text_top,
    coded_out,
    coded_in,
    stats,
    stat_slots,
    warmth_ref,
    offset_ref,
    local_sem,
    send_sem,
    recv_sem,
):
    group, member = lax.axis_index("grp"), lax.axis_index("mem")
    core, x, z_high = lax.rem(group, 2), lax.rem(group // 2, NX), group // (2 * NX)
    y, z_low = lax.rem(member, NY), member // NY
    z = z_high * 2 + z_low

    def device(dx=0, dy=0, dz=0, dc=0):
        to_x, to_y = lax.rem(x + dx + NX, NX), lax.rem(y + dy + NY, NY)
        to_z, to_c = lax.rem(z + dz + NZ, NZ), lax.rem(core + dc, 2)
        return ((to_z // 2 * NX + to_x) * 2 + to_c, lax.rem(to_z, 2) * NY + to_y)

    ahead = {"x": device(dx=1), "y": device(dy=1), "z": device(dz=1)}
    behind = {"x": device(dx=-1), "y": device(dy=-1), "z": device(dz=-1)}
    beyond = {"x": device(dx=2), "y": device(dy=2)}
    other = device(dc=1)

    own_image = pltpu.make_async_copy(
        image_hbm, image.at[pl.ds(IMAGE_AT[0, 0], ROWS)], local_sem.at[0]
    )
    own_text = pltpu.make_async_copy(
        text_hbm, text.at[pl.ds(TEXT_AT[0, 0, 0], ROWS)], local_sem.at[1]
    )
    scalars = [
        pltpu.make_async_copy(warmth_hbm, warmth_ref, local_sem.at[2]),
        pltpu.make_async_copy(offset_hbm, offset_ref, local_sem.at[3]),
    ]
    own_image.start()
    own_text.start()
    for copy in scalars:
        copy.start()

    partners = [other]
    partners += [device(dx=d) for d in range(1, NX)]
    partners += [device(dy=d) for d in range(1, NY)]
    partners += [device(dz=d) for d in range(1, NZ)]
    barrier = pltpu.get_barrier_semaphore()
    for partner in partners:
        pl.semaphore_signal(barrier, inc=1, device_id=partner, device_id_type=MESH)
    pl.semaphore_wait(barrier, len(partners))

    recv_of, sent_of = {}, {}

    def place(key):
        return recv_sem.at[recv_of.setdefault(key, len(recv_of))]

    def send(kind, amount, source, target, to, key):
        at = list(sent_of).index(kind) if kind in sent_of else len(sent_of)
        sent_of[kind] = sent_of.get(kind, 0) + amount
        pltpu.make_async_remote_copy(
            src_ref=source,
            dst_ref=target,
            send_sem=send_sem.at[at],
            recv_sem=place(key),
            device_id=to,
            device_id_type=MESH,
        ).start()

    def expect(key, ref):
        pltpu.make_async_remote_copy(
            src_ref=ref,
            dst_ref=ref,
            send_sem=send_sem.at[0],
            recv_sem=place(key),
            device_id=other,
            device_id_type=MESH,
        ).wait_recv()

    def all_sent(refs):
        for at, (kind, amount) in enumerate(sent_of.items()):
            ref = refs[kind].at[pl.ds(0, amount)]
            pltpu.make_async_remote_copy(
                src_ref=ref,
                dst_ref=ref,
                send_sem=send_sem.at[at],
                recv_sem=recv_sem.at[0],
                device_id=other,
                device_id_type=MESH,
            ).wait_send()

    def axis_of(h, nth):
        return "xy"[(h + nth) % 2]

    tasks = {}

    def send_text(h, i, j, row, rows, nth, step):
        there = (h, (i - step) % 4, j) if nth == 0 else (h, i, (j - step) % 4)
        send(
            "text",
            rows,
            text.at[pl.ds(TEXT_AT[h, i, j] + row, rows)],
            text.at[pl.ds(TEXT_AT[there] + row, rows)],
            {1: ahead, -1: behind, 2: beyond}[step][axis_of(h, nth)],
            ("text", *there),
        )

    def spread(h, i, j, nth):
        send_text(h, i, j, 0, HALF, nth, 1)
        send_text(h, i, j, 0, HALF, nth, -1)

    def on_text(h, i, j):
        expect(("text", h, i, j), text.at[pl.ds(0, HALF)])
        if j == 0:
            spread(h, i, j, 1)
            if i == 2:
                send_text(h, i, j, 0, HALF, 1, 2)
        elif j == 3 and i != 2:
            send_text(h, i, j, 0, QUARTER, 1, 1)
        elif j == 1 and i != 2:
            send_text(h, i, j, QUARTER, QUARTER, 1, -1)

    for h in (0, 1):
        for i in range(4):
            for j in range(4):
                if i or j:
                    tasks["t", h, i, j] = lambda a=(h, i, j): on_text(*a)

    def send_image(d, row, rows, to, there, key):
        send(
            "image",
            rows,
            image.at[pl.ds(IMAGE_AT[0, d] + row, rows)],
            image.at[pl.ds(IMAGE_AT[there] + row, rows)],
            to,
            key,
        )

    def across(d, row, rows):
        part = next(n for n, p in enumerate(PARTS) if d in p)
        send_image(d, row, rows, other, (1, d), ("across", part))

    def along_z(d, row, step):
        there = (d - step) % NZ
        to = (ahead if step == 1 else behind)["z"]
        send_image(d, row, QUARTER, to, (0, there), ("z", there, row))

    def on_image(d, row):
        expect(("z", d, row), image.at[pl.ds(0, QUARTER)])
        if d > 5 or (d == 5 and row < HALF):
            along_z(d, row, 1)
        if d < 3 or (d == 3 and row >= HALF):
            along_z(d, row, -1)
        if row % HALF == (QUARTER if d >= 4 and not (d == 4 and row >= HALF) else 0):
            across(d, row - row % HALF, HALF)

    for d in range(1, NZ):
        for row in range(0, ROWS, QUARTER):
            tasks["z", d, row] = lambda a=(d, row): on_image(*a)
    for n in range(len(PARTS)):
        tasks["c", n] = lambda n=n: expect(
            ("across", n), image.at[pl.ds(0, ROWS * 2)]
        )

    def begin():
        own_text.wait()
        for h in (0, 1):
            spread(h, 0, 0, 0)
        own_image.wait()
        for row in range(0, ROWS, QUARTER):
            along_z(0, row, 1)
            along_z(0, ROWS - QUARTER - row, -1)
        for h in (0, 1):
            send_text(h, 0, 0, 0, HALF, 0, 2)
        for h in (0, 1):
            spread(h, 0, 0, 1)
        across(0, 0, ROWS)
        mine = jnp.broadcast_to(labels_ref[pl.ds(member // 2, 1), :], (8, LANES))
        turned = pltpu.roll(mine, ROWS, 1)
        in_upper = jnp.broadcast_to(lax.rem(member, 2), (8, LANES)) == 1
        labels[0, 0] = jnp.where((lane >= ROWS) == in_upper, mine, turned)
        for d in range(1, NZ):
            there = labels.at[0, NZ - d]
            send("label", 1, labels.at[0, 0], there, device(dz=d), "label")
        for n in range(3):
            stats[n] = zero

    def on_label():
        expect("label", labels.at[0, pl.ds(1, NZ - 1)])
        here, there = labels.at[pl.ds(0, 1)], labels.at[pl.ds(1, 1)]
        send("labels", 1, here, there, other, "labels")

    def on_labels():
        expect("labels", labels.at[pl.ds(0, 1)])
        for at in range(0, TILE // ROWS, 2):
            label_row[:, at * ROWS : (at + 2) * ROWS] = jnp.where(
                lane < ROWS, labels[IMAGE_ORDER[at]], labels[IMAGE_ORDER[at + 1]]
            )

    for copy in scalars:
        copy.wait()
    lane = lax.broadcasted_iota(jnp.int32, (8, LANES), 1)
    zero = jnp.zeros((8, LANES), jnp.float32)
    warmth = jnp.exp(jnp.full((1, 1), warmth_ref[0], jnp.float32))
    offset = offset_ref[0]
    stretch = warmth * (1.0 / PAIRS)
    tasks["begin"] = begin
    tasks["label"] = on_label
    tasks["labels"] = on_labels

    def pairs(chunk, side):
        first, left = chunk * 256, side * 512
        slot = (chunk + side) % 2
        scores[slot] = lax.dot_general(
            text[pl.ds(first, 256), :],
            image[pl.ds(left, 512), :],
            (((1,), (1,)), ((), ())),
            preferred_element_type=jnp.float32,
        )
        for row in range(0, 256, HALF):
            h, i, j = TEXT_HALVES[(first + row) // HALF]
            rx, ry = (i, j) if h == 0 else (j, i)
            owner_x, owner_y = lax.rem(x + rx, NX), lax.rem(y + ry, NY)
            base = (
                ((z_high * NX + owner_x) * 2 + core) * 8 + z_low * NY + owner_y
            ) * ROWS + h * HALF
            position = lax.broadcasted_iota(jnp.int32, (HALF, 1), 0) + base
            for column in (0, 256):
                s = scores[slot, pl.ds(row, HALF), pl.ds(column, 256)]
                logit = s * warmth + offset
                matched = label_row[0:1, pl.ds(left + column, 256)] == position
                signed = jnp.where(matched, -logit, logit)
                e = jnp.exp(-jnp.abs(signed))
                one_e = 1.0 + e
                inverse = 1.0 / one_e
                chance = jnp.where(signed >= 0, inverse, e * inverse)
                factor = jnp.where(matched, -chance, chance)
                coef[pl.ds(first + row, HALF), pl.ds(left + column, 256)] = factor.astype(
                    jnp.bfloat16
                )
                grown = zero
                for r in range(0, HALF, 8):
                    for c in range(0, 256, LANES):
                        piece = slice(r, r + 8), slice(c, c + LANES)
                        grown = grown * one_e[piece] + e[piece]
                stats[0] += fold(jnp.maximum(signed, 0.0)) + jnp.log1p(grown)
                stats[1] += fold(factor * s)
                stats[2] += fold(factor)

    def find_tops(sums, tops, first):
        for row in range(first, first + 256, HALF):
            top = None
            for r in range(0, HALF, 8):
                for c in range(0, D, LANES):
                    part = jnp.abs(sums[pl.ds(row + r, 8), c : c + LANES])
                    top = part if top is None else jnp.maximum(top, part)
            top = jnp.max(jnp.max(top, axis=1, keepdims=True), axis=0, keepdims=True)
            power = jnp.ceil(jnp.log2(jnp.maximum(top, SMALLEST)))
            tops[row // HALF] = jnp.broadcast_to(power, (QUARTER, LANES))

    def text_part(chunk):
        at = pl.ds(chunk * 256, 256)
        text_sum[at, :] = jnp.dot(
            coef[at, :], image[...], preferred_element_type=jnp.float32
        )
        find_tops(text_sum, text_top, chunk * 256)

    def image_part(chunk):
        at = pl.ds(chunk * 256, 256)
        image_sum[at, :] = lax.dot_general(
            coef[:, at],
            text[...],
            (((0,), (0,)), ((), ())),
            preferred_element_type=jnp.float32,
        )
        find_tops(image_sum, image_top, chunk * 256)

    messages = {}
    used = [0]

    def arrived(parts):
        found = {}
        for adds in parts:
            for name, _ in adds:
                if name not in found:
                    power = coded_in[messages[name]].astype(jnp.float32)
                    found[name] = jnp.exp2(power) * (1.0 / LEVELS), power
        return found

    def summed(sums, row, wide, adds, found):
        value = sums[pl.ds(row, QUARTER), wide * LANES : (wide + 1) * LANES]
        for name, nth in adds:
            tile = coded_in[messages[name] + 1 + nth * WIDE + wide]
            value = value + tile.astype(jnp.float32) * found[name][0]
        return value

    def send_sums(*sending):
        ready = []
        for name, sums, tops, row, parts, to, key in sending:
            start, count = used[0], 1 + len(parts) * WIDE
            messages[name] = start
            used[0] += count
            found = arrived(parts)
            powers = [tops[row // HALF]]
            if len(parts) * QUARTER > HALF:
                powers[0] = jnp.maximum(powers[0], tops[row // HALF + 1])
            powers += [power for _, power in found.values()]
            while len(powers) > 1:
                powers = powers[2:] + [jnp.maximum(powers[0], powers[1]) + 1.0]
            coded_out[start] = powers[0].astype(jnp.int16)
            scale = jnp.exp2(-powers[0]) * LEVELS
            for n, adds in enumerate(parts):
                for wide in range(WIDE):
                    value = summed(sums, row + n * QUARTER, wide, adds, found)
                    coded_out[start + 1 + n * WIDE + wide] = (
                        jnp.round(value * scale).astype(jnp.int32).astype(jnp.int16)
                    )
            ready.append((pl.ds(start, count), count, to, key))
        for at, count, to, key in ready:
            send("sum", count, coded_out.at[at], coded_in.at[at], to, key)

    def await_sum(key, *sizes):
        count = sum(1 + rows // QUARTER * WIDE for rows in sizes)
        expect(key, coded_in.at[pl.ds(0, count)])

    def direct(i):
        return i == 0

    def second_far(i):
        sending = []
        for h in (0, 1):
            axis, at = axis_of(h, 1), TEXT_AT[h, i, 2]
            if direct(i):
                name, to = (h, i, "far"), beyond[axis]
                sending.append(
                    (name, text_sum, text_top, at, [[], []], to, (h, i, "n"))
                )
                continue
            for far, row, to in (("fa", 0, ahead), ("fb", QUARTER, behind)):
                name = (h, i, far)
                sending.append(
                    (name, text_sum, text_top, at + row, [[]], to[axis], name)
                )
        send_sums(*sending)

    def second_near(i):
        sending = []
        for h in (0, 1):
            for j, far, near, to in ((1, "fa", "na", ahead), (3, "fb", "nb", behind)):
                parts = [[], []]
                if not direct(i):
                    await_sum((h, i, far), QUARTER)
                    parts[j == 3].append(((h, i, far), 0))
                at, to = TEXT_AT[h, i, j], to[axis_of(h, 1)]
                name = (h, i, near)
                sending.append((name, text_sum, text_top, at, parts, to, (h, i, "n")))
        send_sums(*sending)

    def line(h, i, nth):
        adds = [((h, i, "na"), nth), ((h, i, "nb"), nth)]
        return adds + [((h, i, "far"), nth)] if direct(i) else adds

    def first(i):
        sending = []
        for h in (0, 1):
            await_sum((h, i, "n"), *[HALF] * (3 if direct(i) else 2))
            to = {1: ahead, 2: beyond, 3: behind}[i][axis_of(h, 0)]
            parts = [line(h, i, 0), line(h, i, 1)]
            at = TEXT_AT[h, i, 0]
            sending.append(((h, "n", i), text_sum, text_top, at, parts, to, (h, "n")))
        send_sums(*sending)

    def text_last(h):
        await_sum((h, 0, "n"), *[HALF] * (3 if direct(0) else 2))
        await_sum((h, "n"), HALF, HALF, HALF)
        for n in (0, 1):
            adds = line(h, 0, n) + [((h, "n", i), n) for i in (1, 2, 3)]
            found = arrived([adds])
            at = h * HALF + n * QUARTER
            row = TEXT_AT[h, 0, 0] + n * QUARTER
            for wide in range(WIDE):
                value = summed(text_sum, row, wide, adds, found)
                text_out[at : at + QUARTER, wide * LANES : (wide + 1) * LANES] = (
                    value * stretch
                )

    for i in range(4):
        tasks["sf", i] = lambda i=i: second_far(i)
        tasks["sn", i] = lambda i=i: second_near(i)
        if i:
            tasks["f", i] = lambda i=i: first(i)
    for h in (0, 1):
        tasks["tl", h] = lambda h=h: text_last(h)

    def to_other(n):
        sending = []
        for d in PARTS[n]:
            parts = [[] for _ in range(4)]
            at = IMAGE_AT[1, d]
            sending.append((("c", d), image_sum, image_top, at, parts, other, ("c", d)))
        send_sums(*sending)

    def z_adds(d, row):
        adds = [(("c", d), row // QUARTER)]
        if d < 4 and (d < 3 or row < HALF):
            adds.append((("za", d + 1, row), 0))
        if (d > 4 or d == 0) and (d != 5 or row >= HALF):
            adds.append((("zb", (d - 1) % NZ, row), 0))
        return adds

    def z_send(far, row):
        sending = []
        for d, r, way, to in (
            (far, row, "za", ahead),
            (NZ - far, ROWS - QUARTER - row, "zb", behind),
        ):
            adds = z_adds(d, r)
            for name, _ in adds[1:]:
                await_sum(name, QUARTER)
            name, at = (way, d, r), IMAGE_AT[0, d] + r
            sending.append((name, image_sum, image_top, at, [adds], to["z"], name))
        send_sums(*sending)

    def image_last(row):
        adds = z_adds(0, row)
        for name, _ in adds[1:]:
            await_sum(name, QUARTER)
        found = arrived([adds])
        for wide in range(WIDE):
            value = summed(image_sum, IMAGE_AT[0, 0] + row, wide, adds, found)
            image_out[row : row + QUARTER, wide * LANES : (wide + 1) * LANES] = (
                value * stretch
            )

    for n in range(4):
        tasks["co", n] = lambda n=n: to_other(n)
        tasks["T", n] = lambda n=n: text_part(n)
        tasks["I", n] = lambda n=n: image_part(n)
        for chunk in range(4):
            if n < 2:
                tasks["p", chunk, n] = lambda a=(chunk, n): pairs(*a)
    for d in range(NZ):
        tasks["cw", d] = lambda d=d: await_sum(("c", d), ROWS)
        for row in range(0, ROWS, QUARTER):
            if d == 0:
                tasks["zl", row] = lambda row=row: image_last(row)
            elif d < 4 or (d == 4 and row < HALF):
                tasks["zs", d, row] = lambda a=(d, row): z_send(*a)

    stat_axes = (
        (2, core, lambda d: device(dc=d)),
        (NX, x, lambda d: device(dx=d)),
        (NY, y, lambda d: device(dy=d)),
        (NZ, z, lambda d: device(dz=d)),
    )

    def stat_send(nth, value):
        base = sum(a[0] for a in stat_axes[:nth])
        size, me, to = stat_axes[nth]
        stat_slots[base + me] = value
        for d in range(1, size):
            slot = stat_slots.at[pl.ds(base + me, 1)]
            send("stat", 1, slot, slot, to(d), ("stat", nth))

    def stat_sum(nth):
        base, size = sum(a[0] for a in stat_axes[:nth]), stat_axes[nth][0]
        expect(("stat", nth), stat_slots.at[pl.ds(0, size - 1)])
        value = stat_slots[base]
        for n in range(1, size):
            value = value + stat_slots[base + n]
        return value

    def first_stats():
        rows = [jnp.sum(stats[n], axis=0, keepdims=True) for n in range(3)]
        rows.append(jnp.zeros((5, LANES), jnp.float32))
        stat_send(0, jnp.concatenate(rows, axis=0))

    def last_stats():
        everyone = stat_sum(3)
        share = 1.0 / float(PAIRS * PAIRS)
        stats_out[0] = jnp.sum(everyone[0:1, :]) * share
        stats_out[1] = jnp.sum(everyone[1:2, :] * warmth) * share
        stats_out[2] = jnp.sum(everyone[2:3, :]) * share

    tasks["s", 0] = first_stats
    for n in (1, 2, 3):
        tasks["s", n] = lambda n=n: stat_send(n, stat_sum(n - 1))
    tasks["s", 4] = last_stats

    for task in ORDER:
        tasks[task]()
    all_sent(
        {
            "text": text,
            "image": image,
            "label": labels.at[0],
            "labels": labels,
            "sum": coded_out,
            "stat": stat_slots,
        }
    )


def on_device(picture, caption, labels, warmth, offset):
    vmem = pl.BlockSpec(memory_space=pltpu.VMEM)
    smem = pl.BlockSpec(memory_space=pltpu.SMEM)
    hbm = pl.BlockSpec(memory_space=pl.ANY)
    grad = pltpu.VMEM((ROWS, D), jnp.float32)
    return pl.pallas_call(
        kernel,
        out_shape=(grad, grad, jax.ShapeDtypeStruct((3,), jnp.float32)),
        in_specs=[hbm, hbm, vmem, hbm, hbm],
        out_specs=(vmem, vmem, smem),
        scratch_shapes=[
            pltpu.VMEM((TILE, D), jnp.bfloat16),
            pltpu.VMEM((TILE, D), jnp.bfloat16),
            pltpu.VMEM((2, NZ, 8, LANES), jnp.int32),
            pltpu.VMEM((8, TILE), jnp.int32),
            pltpu.VMEM((2, 256, 512), jnp.float32),
            pltpu.VMEM((TILE, TILE), jnp.bfloat16),
            pltpu.VMEM((TILE, D), jnp.float32),
            pltpu.VMEM((TILE, D), jnp.float32),
            pltpu.VMEM((TILE // HALF, QUARTER, LANES), jnp.float32),
            pltpu.VMEM((TILE // HALF, QUARTER, LANES), jnp.float32),
            pltpu.VMEM((N_TILES, QUARTER, LANES), jnp.int16),
            pltpu.VMEM((N_TILES, QUARTER, LANES), jnp.int16),
            pltpu.VMEM((3, 8, LANES), jnp.float32),
            pltpu.VMEM((2 + NX + NY + NZ, 8, LANES), jnp.float32),
            pltpu.SMEM((1,), jnp.float32),
            pltpu.SMEM((1,), jnp.float32),
            pltpu.SemaphoreType.DMA((4,)),
            pltpu.SemaphoreType.DMA((N_SEND,)),
            pltpu.SemaphoreType.DMA((N_RECV,)),
        ],
        compiler_params=pltpu.CompilerParams(
            collective_id=0, has_side_effects=True, vmem_limit_bytes=56 << 20
        ),
    )(warmth, offset, labels.reshape(4, LANES), picture, caption)


def solution(mesh):
    rows = P(("grp", "mem"), None)
    return jax.shard_map(
        on_device,
        mesh=mesh,
        in_specs=(rows, rows, P("grp"), P(), P()),
        out_specs=(rows, rows, P()),
        check_vma=False,
    )
```

```python
import jax
import jax.numpy as jnp
from jax import lax
from jax.experimental import pallas as pl
from jax.experimental.pallas import tpu as pltpu
from jax.sharding import PartitionSpec as P

MESH = pl.DeviceIdType.MESH
NX, NY, NZ = 4, 4, 8
ROWS = 64
HALF, QUARTER = 32, 16
D = 1152
LANES = 128
WIDE = D // LANES
TILE = 1024
PAIRS = 16384
LEVELS = 32000.0
SMALLEST = 1e-30

FAR_FIRST = (2, 1, 3, 0)
TEXT_HALVES = [
    (h, i, j)
    for i in FAR_FIRST
    for h in (0, 1)
    for j in (FAR_FIRST if h == 0 else FAR_FIRST[::-1])
]
TEXT_AT = {key: n * HALF for n, key in enumerate(TEXT_HALVES)}
PARTS = ((4, 3), (5, 2), (6, 1), (7, 0))
IMAGE_ORDER = [(c, d) for part in PARTS for c in (1, 0) for d in part]
IMAGE_AT = {key: n * ROWS for n, key in enumerate(IMAGE_ORDER)}
N_SEND, N_RECV = 6, 128
N_TILES = 1152
ORDER = [
    "begin", ("z", 7, 0), ("z", 1, 48), ("t", 0, 1, 0), ("t", 1, 3, 0), ("z", 1, 32), ("t", 1, 1, 0),
    ("z", 7, 16), ("z", 1, 16), ("t", 0, 3, 0), ("z", 7, 32), ("z", 1, 0), ("t", 1, 2, 0), ("z", 7, 48),
    ("t", 0, 2, 0), ("t", 1, 0, 3), ("t", 1, 0, 1), ("z", 6, 0), ("z", 2, 48), "label", ("z", 6, 16),
    ("t", 1, 3, 3), ("z", 2, 32), ("t", 0, 0, 3), ("t", 0, 0, 1), ("t", 0, 1, 3), ("z", 6, 32), ("z", 2, 16),
    ("t", 0, 1, 1), ("t", 0, 3, 3), ("t", 1, 3, 1), ("z", 6, 48), ("z", 2, 0), ("z", 5, 0), ("t", 0, 3, 1),
    ("t", 1, 1, 1), ("z", 3, 48), ("c", 3), ("t", 1, 1, 3), ("t", 1, 2, 1), ("t", 0, 2, 1), ("c", 2),
    ("z", 5, 16), ("t", 0, 2, 3), ("z", 3, 32), ("t", 1, 2, 3), "far", ("t", 1, 2, 2), ("t", 0, 2, 2),
    ("t", 0, 0, 2), ("t", 1, 0, 2), "labels", ("p", 0, 1), ("p", 3, 1), ("t", 1, 3, 2), ("t", 0, 1, 2),
    ("z", 5, 32), ("z", 5, 48), ("t", 0, 3, 2), ("p", 2, 1), ("z", 4, 48), ("z", 3, 16), ("z", 3, 0),
    ("z", 4, 0), ("z", 4, 16), ("c", 1), ("t", 1, 1, 2), ("z", 4, 32), ("p", 1, 1), ("T", 1, "a"),
    ("T", 2, "a"), ("c", 0), ("p", 1, 0), ("p", 3, 0), ("p", 2, 0), ("p", 0, 0), ("s", 0), ("I", 0, "b"),
    ("co", 0), ("T", 0, "b"), ("sf", 2), ("I", 1, "b"), ("cw", 4), ("zs", 4, 0), ("co", 1), ("s", 1),
    ("zs", 4, 16), ("T", 1, "b"), ("sf", 1), ("cw", 3), ("I", 2, "a"), ("cw", 5), ("zs", 3, 32),
    ("T", 2, "b"), ("sf", 3), ("zs", 3, 48), ("sn", 2), ("cw", 2), ("s", 2), ("zs", 3, 0), ("I", 2, "b"),
    ("co", 2), ("zs", 3, 16), ("I", 3, "a"), ("sn", 1), ("I", 3, "b"), ("cw", 6), ("zs", 2, 32), ("co", 3),
    ("zs", 2, 48), ("sn", 3), ("s", 3), ("zs", 2, 0), ("T", 3, "a"), ("zs", 2, 16), ("f", 2), ("cw", 7),
    ("T", 3, "b"), ("sf", 0), ("sn", 0), ("cw", 0), ("cw", 1), ("zs", 1, 32), ("zs", 1, 48), ("s", "z"),
    ("zs", 1, 0), ("f", 1), ("f", 3), ("zs", 1, 16), ("zl", 0), ("zl", 48), ("zl", 32), ("s", 4), ("zl", 16),
    ("tl", 0), ("tl", 1),
]


def fold(values):
    rows, columns = values.shape
    parts = [
        values[r : r + 8, c : c + LANES]
        for r in range(0, rows, 8)
        for c in range(0, columns, LANES)
    ]
    while len(parts) > 1:
        parts = [a + b for a, b in zip(parts[::2], parts[1::2], strict=True)]
    return parts[0]


def kernel(
    warmth_hbm,
    offset_hbm,
    labels_ref,
    image_hbm,
    text_hbm,
    image_out,
    text_out,
    stats_out,
    image,
    text,
    labels,
    label_row,
    scores,
    coef,
    image_sum,
    text_sum,
    image_top,
    text_top,
    coded_out,
    coded_in,
    stats,
    stat_slots,
    warmth_ref,
    offset_ref,
    local_sem,
    send_sem,
    recv_sem,
):
    group, member = lax.axis_index("grp"), lax.axis_index("mem")
    core, x, z_high = lax.rem(group, 2), lax.rem(group // 2, NX), group // (2 * NX)
    y, z_low = lax.rem(member, NY), member // NY
    z = z_high * 2 + z_low

    def device(dx=0, dy=0, dz=0, dc=0):
        to_x, to_y = lax.rem(x + dx + NX, NX), lax.rem(y + dy + NY, NY)
        to_z, to_c = lax.rem(z + dz + NZ, NZ), lax.rem(core + dc, 2)
        return ((to_z // 2 * NX + to_x) * 2 + to_c, lax.rem(to_z, 2) * NY + to_y)

    ahead = {"x": device(dx=1), "y": device(dy=1), "z": device(dz=1)}
    behind = {"x": device(dx=-1), "y": device(dy=-1), "z": device(dz=-1)}
    beyond = {"x": device(dx=2), "y": device(dy=2)}
    other = device(dc=1)
    near_steps, relays = (1, -1, 2, -2), ((6, 1), (6, 2), (2, -1))

    own_image = pltpu.make_async_copy(
        image_hbm, image.at[pl.ds(IMAGE_AT[0, 0], ROWS)], local_sem.at[0]
    )
    own_text = pltpu.make_async_copy(
        text_hbm, text.at[pl.ds(TEXT_AT[0, 0, 0], ROWS)], local_sem.at[1]
    )
    scalars = [
        pltpu.make_async_copy(warmth_hbm, warmth_ref, local_sem.at[2]),
        pltpu.make_async_copy(offset_hbm, offset_ref, local_sem.at[3]),
    ]
    own_image.start()
    own_text.start()
    for copy in scalars:
        copy.start()

    partners = [other]
    partners += [device(dx=d) for d in range(1, NX)]
    partners += [device(dy=d) for d in range(1, NY)]
    partners += [device(dz=d) for d in near_steps]
    barrier = pltpu.get_barrier_semaphore()
    for partner in partners:
        pl.semaphore_signal(barrier, inc=1, device_id=partner, device_id_type=MESH)
    pl.semaphore_wait(barrier, len(partners))

    recv_of, sent_of = {}, {}

    def place(key):
        return recv_sem.at[recv_of.setdefault(key, len(recv_of))]

    def send(kind, amount, source, target, to, key):
        at = list(sent_of).index(kind) if kind in sent_of else len(sent_of)
        sent_of[kind] = sent_of.get(kind, 0) + amount
        pltpu.make_async_remote_copy(
            src_ref=source,
            dst_ref=target,
            send_sem=send_sem.at[at],
            recv_sem=place(key),
            device_id=to,
            device_id_type=MESH,
        ).start()

    def expect(key, ref):
        pltpu.make_async_remote_copy(
            src_ref=ref,
            dst_ref=ref,
            send_sem=send_sem.at[0],
            recv_sem=place(key),
            device_id=other,
            device_id_type=MESH,
        ).wait_recv()

    def all_sent(refs):
        for at, (kind, amount) in enumerate(sent_of.items()):
            ref = refs[kind].at[pl.ds(0, amount)]
            pltpu.make_async_remote_copy(
                src_ref=ref,
                dst_ref=ref,
                send_sem=send_sem.at[at],
                recv_sem=recv_sem.at[0],
                device_id=other,
                device_id_type=MESH,
            ).wait_send()

    def axis_of(h, nth):
        return "xy"[(h + nth) % 2]

    tasks = {}

    def send_text(h, i, j, row, rows, nth, step):
        there = (h, (i - step) % 4, j) if nth == 0 else (h, i, (j - step) % 4)
        send(
            "text",
            rows,
            text.at[pl.ds(TEXT_AT[h, i, j] + row, rows)],
            text.at[pl.ds(TEXT_AT[there] + row, rows)],
            {1: ahead, -1: behind, 2: beyond}[step][axis_of(h, nth)],
            ("text", *there),
        )

    def spread(h, i, j, nth):
        send_text(h, i, j, 0, HALF, nth, 1)
        send_text(h, i, j, 0, HALF, nth, -1)

    def on_text(h, i, j):
        expect(("text", h, i, j), text.at[pl.ds(0, HALF)])
        if j == 0:
            spread(h, i, j, 1)
            if i == 2:
                send_text(h, i, j, 0, HALF, 1, 2)
        elif j == 3 and i != 2:
            send_text(h, i, j, 0, QUARTER, 1, 1)
        elif j == 1 and i != 2:
            send_text(h, i, j, QUARTER, QUARTER, 1, -1)

    for h in (0, 1):
        for i in range(4):
            for j in range(4):
                if i or j:
                    tasks["t", h, i, j] = lambda a=(h, i, j): on_text(*a)

    def send_image(d, row, rows, to, there, key):
        send(
            "image",
            rows,
            image.at[pl.ds(IMAGE_AT[0, d] + row, rows)],
            image.at[pl.ds(IMAGE_AT[there] + row, rows)],
            to,
            key,
        )

    def across(d, row, rows):
        part = next(n for n, p in enumerate(PARTS) if d in p)
        send_image(d, row, rows, other, (1, d), ("across", part))

    def along_z(d, row, step):
        there = (d - step) % NZ
        to = (ahead if step == 1 else behind)["z"]
        send_image(d, row, QUARTER, to, (0, there), ("z", there, row))

    def on_image(d, row):
        expect(("z", d, row), image.at[pl.ds(0, QUARTER)])
        if d > 5 or (d == 5 and row < HALF):
            along_z(d, row, 1)
        if d < 3 or (d == 3 and row >= HALF):
            along_z(d, row, -1)
        if row % HALF == (QUARTER if d >= 4 and not (d == 4 and row >= HALF) else 0):
            across(d, row - row % HALF, HALF)

    for d in range(1, NZ):
        for row in range(0, ROWS, QUARTER):
            tasks["z", d, row] = lambda a=(d, row): on_image(*a)
    for n in range(len(PARTS)):
        tasks["c", n] = lambda n=n: expect(
            ("across", n), image.at[pl.ds(0, ROWS * 2)]
        )

    def begin():
        own_text.wait()
        for h in (0, 1):
            spread(h, 0, 0, 0)
        own_image.wait()
        for row in range(0, ROWS, QUARTER):
            along_z(0, row, 1)
            along_z(0, ROWS - QUARTER - row, -1)
        for h in (0, 1):
            send_text(h, 0, 0, 0, HALF, 0, 2)
        for h in (0, 1):
            spread(h, 0, 0, 1)
        across(0, 0, ROWS)
        mine = jnp.broadcast_to(labels_ref[pl.ds(member // 2, 1), :], (8, LANES))
        turned = pltpu.roll(mine, ROWS, 1)
        in_upper = jnp.broadcast_to(lax.rem(member, 2), (8, LANES)) == 1
        labels[0, 0] = jnp.where((lane >= ROWS) == in_upper, mine, turned)
        for d in near_steps:
            there = labels.at[0, -d % NZ]
            send("label", 1, labels.at[0, 0], there, device(dz=d), "label")
        for n in range(3):
            stats[n] = zero

    def on_label():
        expect("label", labels.at[0, pl.ds(0, len(near_steps))])
        for d, step in relays:
            here, there = labels.at[0, d], labels.at[0, (d - step) % NZ]
            send("label", 1, here, there, device(dz=step), "far")

    def on_far_label():
        expect("far", labels.at[0, pl.ds(0, len(relays))])
        here, there = labels.at[pl.ds(0, 1)], labels.at[pl.ds(1, 1)]
        send("labels", 1, here, there, other, "labels")

    def on_labels():
        expect("labels", labels.at[pl.ds(0, 1)])
        for at in range(0, TILE // ROWS, 2):
            label_row[:, at * ROWS : (at + 2) * ROWS] = jnp.where(
                lane < ROWS, labels[IMAGE_ORDER[at]], labels[IMAGE_ORDER[at + 1]]
            )

    for copy in scalars:
        copy.wait()
    lane = lax.broadcasted_iota(jnp.int32, (8, LANES), 1)
    zero = jnp.zeros((8, LANES), jnp.float32)
    warmth = jnp.exp(jnp.full((1, 1), warmth_ref[0], jnp.float32))
    offset = offset_ref[0]
    stretch = warmth * (1.0 / PAIRS)
    tasks["begin"] = begin
    tasks["label"] = on_label
    tasks["far"] = on_far_label
    tasks["labels"] = on_labels

    def pairs(chunk, side):
        first, left = chunk * 256, side * 512
        slot = (chunk + side) % 2
        scores[slot] = lax.dot_general(
            text[pl.ds(first, 256), :],
            image[pl.ds(left, 512), :],
            (((1,), (1,)), ((), ())),
            preferred_element_type=jnp.float32,
        )
        for row in range(0, 256, HALF):
            h, i, j = TEXT_HALVES[(first + row) // HALF]
            rx, ry = (i, j) if h == 0 else (j, i)
            owner_x, owner_y = lax.rem(x + rx, NX), lax.rem(y + ry, NY)
            base = (
                ((z_high * NX + owner_x) * 2 + core) * 8 + z_low * NY + owner_y
            ) * ROWS + h * HALF
            position = lax.broadcasted_iota(jnp.int32, (HALF, 1), 0) + base
            for column in (0, 256):
                s = scores[slot, pl.ds(row, HALF), pl.ds(column, 256)]
                logit = s * warmth + offset
                matched = label_row[0:1, pl.ds(left + column, 256)] == position
                signed = jnp.where(matched, -logit, logit)
                e = jnp.exp(-jnp.abs(signed))
                one_e = 1.0 + e
                inverse = 1.0 / one_e
                chance = jnp.where(signed >= 0, inverse, e * inverse)
                factor = jnp.where(matched, -chance, chance)
                coef[pl.ds(first + row, HALF), pl.ds(left + column, 256)] = factor.astype(
                    jnp.bfloat16
                )
                grown = zero
                for r in range(0, HALF, 8):
                    for c in range(0, 256, LANES):
                        piece = slice(r, r + 8), slice(c, c + LANES)
                        grown = grown * one_e[piece] + e[piece]
                stats[0] += fold(jnp.maximum(signed, 0.0)) + jnp.log1p(grown)
                stats[1] += fold(factor * s)
                stats[2] += fold(factor)

    def find_tops(sums, tops, first):
        for row in range(first, first + 256, HALF):
            top = None
            for r in range(0, HALF, 8):
                for c in range(0, D, LANES):
                    part = jnp.abs(sums[pl.ds(row + r, 8), c : c + LANES])
                    top = part if top is None else jnp.maximum(top, part)
            top = jnp.max(jnp.max(top, axis=1, keepdims=True), axis=0, keepdims=True)
            power = jnp.ceil(jnp.log2(jnp.maximum(top, SMALLEST)))
            tops[row // HALF] = jnp.broadcast_to(power, (QUARTER, LANES))

    def text_part(chunk, step):
        at = pl.ds(chunk * 256, 256)
        along = {"a": pl.ds(512, 512), "b": pl.ds(0, 512 if chunk else TILE)}[step]
        product = jnp.dot(
            coef[at, along], image[along, :], preferred_element_type=jnp.float32
        )
        if step == "b" and chunk:
            product = product + text_sum[at, :]
        text_sum[at, :] = product
        if step == "b":
            find_tops(text_sum, text_top, chunk * 256)

    def image_part(part, step):
        at = pl.ds(part * 256, 256)
        rest = part >= 2
        along = {"a": pl.ds(256, 768), "b": pl.ds(0, 256 if rest else TILE)}[step]
        product = lax.dot_general(
            coef[along, at],
            text[along, :],
            (((0,), (0,)), ((), ())),
            preferred_element_type=jnp.float32,
        )
        if step == "b" and rest:
            product = product + image_sum[at, :]
        image_sum[at, :] = product
        if step == "b":
            find_tops(image_sum, image_top, part * 256)

    messages = {}
    used = [0]

    def arrived(parts):
        found = {}
        for adds in parts:
            for name, _ in adds:
                if name not in found:
                    power = coded_in[messages[name]].astype(jnp.float32)
                    found[name] = jnp.exp2(power) * (1.0 / LEVELS), power
        return found

    def summed(sums, row, wide, adds, found):
        value = sums[pl.ds(row, QUARTER), wide * LANES : (wide + 1) * LANES]
        for name, nth in adds:
            tile = coded_in[messages[name] + 1 + nth * WIDE + wide]
            value = value + tile.astype(jnp.float32) * found[name][0]
        return value

    def send_sums(*sending):
        ready = []
        for name, sums, tops, row, parts, to, key in sending:
            start, count = used[0], 1 + len(parts) * WIDE
            messages[name] = start
            used[0] += count
            found = arrived(parts)
            powers = [tops[row // HALF]]
            if len(parts) * QUARTER > HALF:
                powers[0] = jnp.maximum(powers[0], tops[row // HALF + 1])
            powers += [power for _, power in found.values()]
            while len(powers) > 1:
                powers = powers[2:] + [jnp.maximum(powers[0], powers[1]) + 1.0]
            coded_out[start] = powers[0].astype(jnp.int16)
            scale = jnp.exp2(-powers[0]) * LEVELS
            for n, adds in enumerate(parts):
                for wide in range(WIDE):
                    value = summed(sums, row + n * QUARTER, wide, adds, found)
                    coded_out[start + 1 + n * WIDE + wide] = (
                        jnp.round(value * scale).astype(jnp.int32).astype(jnp.int16)
                    )
            ready.append((pl.ds(start, count), count, to, key))
        for at, count, to, key in ready:
            send("sum", count, coded_out.at[at], coded_in.at[at], to, key)

    def await_sum(key, *sizes):
        count = sum(1 + rows // QUARTER * WIDE for rows in sizes)
        expect(key, coded_in.at[pl.ds(0, count)])

    def direct(i):
        return i == 0

    def second_far(i):
        sending = []
        for h in (0, 1):
            axis, at = axis_of(h, 1), TEXT_AT[h, i, 2]
            if direct(i):
                name, to = (h, i, "far"), beyond[axis]
                sending.append(
                    (name, text_sum, text_top, at, [[], []], to, (h, i, "n"))
                )
                continue
            for far, row, to in (("fa", 0, ahead), ("fb", QUARTER, behind)):
                name = (h, i, far)
                sending.append(
                    (name, text_sum, text_top, at + row, [[]], to[axis], name)
                )
        send_sums(*sending)

    def second_near(i):
        sending = []
        for h in (0, 1):
            for j, far, near, to in ((1, "fa", "na", ahead), (3, "fb", "nb", behind)):
                parts = [[], []]
                if not direct(i):
                    await_sum((h, i, far), QUARTER)
                    parts[j == 3].append(((h, i, far), 0))
                at, to = TEXT_AT[h, i, j], to[axis_of(h, 1)]
                name = (h, i, near)
                sending.append((name, text_sum, text_top, at, parts, to, (h, i, "n")))
        send_sums(*sending)

    def line(h, i, nth):
        adds = [((h, i, "na"), nth), ((h, i, "nb"), nth)]
        return adds + [((h, i, "far"), nth)] if direct(i) else adds

    def first(i):
        sending = []
        for h in (0, 1):
            await_sum((h, i, "n"), *[HALF] * (3 if direct(i) else 2))
            to = {1: ahead, 2: beyond, 3: behind}[i][axis_of(h, 0)]
            parts = [line(h, i, 0), line(h, i, 1)]
            at = TEXT_AT[h, i, 0]
            sending.append(((h, "n", i), text_sum, text_top, at, parts, to, (h, "n")))
        send_sums(*sending)

    def text_last(h):
        await_sum((h, 0, "n"), *[HALF] * (3 if direct(0) else 2))
        await_sum((h, "n"), HALF, HALF, HALF)
        for n in (0, 1):
            adds = line(h, 0, n) + [((h, "n", i), n) for i in (1, 2, 3)]
            found = arrived([adds])
            at = h * HALF + n * QUARTER
            row = TEXT_AT[h, 0, 0] + n * QUARTER
            for wide in range(WIDE):
                value = summed(text_sum, row, wide, adds, found)
                text_out[at : at + QUARTER, wide * LANES : (wide + 1) * LANES] = (
                    value * stretch
                )

    for i in range(4):
        tasks["sf", i] = lambda i=i: second_far(i)
        tasks["sn", i] = lambda i=i: second_near(i)
        if i:
            tasks["f", i] = lambda i=i: first(i)
    for h in (0, 1):
        tasks["tl", h] = lambda h=h: text_last(h)

    def to_other(n):
        sending = []
        for d in PARTS[n]:
            parts = [[] for _ in range(4)]
            at = IMAGE_AT[1, d]
            sending.append((("c", d), image_sum, image_top, at, parts, other, ("c", d)))
        send_sums(*sending)

    def z_adds(d, row):
        adds = [(("c", d), row // QUARTER)]
        if d < 4 and (d < 3 or row < HALF):
            adds.append((("za", d + 1, row), 0))
        if (d > 4 or d == 0) and (d != 5 or row >= HALF):
            adds.append((("zb", (d - 1) % NZ, row), 0))
        return adds

    def z_send(far, row):
        sending = []
        for d, r, way, to in (
            (far, row, "za", ahead),
            (NZ - far, ROWS - QUARTER - row, "zb", behind),
        ):
            adds = z_adds(d, r)
            for name, _ in adds[1:]:
                await_sum(name, QUARTER)
            name, at = (way, d, r), IMAGE_AT[0, d] + r
            sending.append((name, image_sum, image_top, at, [adds], to["z"], name))
        send_sums(*sending)

    def image_last(row):
        adds = z_adds(0, row)
        for name, _ in adds[1:]:
            await_sum(name, QUARTER)
        found = arrived([adds])
        for wide in range(WIDE):
            value = summed(image_sum, IMAGE_AT[0, 0] + row, wide, adds, found)
            image_out[row : row + QUARTER, wide * LANES : (wide + 1) * LANES] = (
                value * stretch
            )

    for n in range(4):
        tasks["co", n] = lambda n=n: to_other(n)
        for step in "ab":
            if step == "b" or n >= 1:
                tasks["T", n, step] = lambda a=(n, step): text_part(*a)
            if step == "b" or n >= 2:
                tasks["I", n, step] = lambda a=(n, step): image_part(*a)
        for chunk in range(4):
            if n < 2:
                tasks["p", chunk, n] = lambda a=(chunk, n): pairs(*a)
    for d in range(NZ):
        tasks["cw", d] = lambda d=d: await_sum(("c", d), ROWS)
        for row in range(0, ROWS, QUARTER):
            if d == 0:
                tasks["zl", row] = lambda row=row: image_last(row)
            elif d < 4 or (d == 4 and row < HALF):
                tasks["zs", d, row] = lambda a=(d, row): z_send(*a)

    stat_axes = (
        (2, core, lambda d: device(dc=d)),
        (NX, x, lambda d: device(dx=d)),
        (NY, y, lambda d: device(dy=d)),
        (NZ, z, lambda d: device(dz=d)),
    )

    def stat_send(nth, value):
        base = sum(a[0] for a in stat_axes[:nth])
        size, me, to = stat_axes[nth]
        stat_slots[base + me] = value
        for d in near_steps if size == NZ else range(1, size):
            slot = stat_slots.at[pl.ds(base + me, 1)]
            send("stat", 1, slot, slot, to(d), ("stat", nth))

    def stat_relay():
        base = 2 + NX + NY
        expect(("stat", 3), stat_slots.at[pl.ds(0, len(near_steps))])
        for d, step in relays:
            slot = stat_slots.at[pl.ds(base + lax.rem(z + d, NZ), 1)]
            send("stat", 1, slot, slot, device(dz=step), ("stat", 4))

    def stat_sum(nth):
        base, size = sum(a[0] for a in stat_axes[:nth]), stat_axes[nth][0]
        if size == NZ:
            expect(("stat", 4), stat_slots.at[pl.ds(0, len(relays))])
        else:
            expect(("stat", nth), stat_slots.at[pl.ds(0, size - 1)])
        value = stat_slots[base]
        for n in range(1, size):
            value = value + stat_slots[base + n]
        return value

    def first_stats():
        rows = [jnp.sum(stats[n], axis=0, keepdims=True) for n in range(3)]
        rows.append(jnp.zeros((5, LANES), jnp.float32))
        stat_send(0, jnp.concatenate(rows, axis=0))

    def last_stats():
        everyone = stat_sum(3)
        share = 1.0 / float(PAIRS * PAIRS)
        stats_out[0] = jnp.sum(everyone[0:1, :]) * share
        stats_out[1] = jnp.sum(everyone[1:2, :] * warmth) * share
        stats_out[2] = jnp.sum(everyone[2:3, :]) * share

    tasks["s", 0] = first_stats
    for n in (1, 2, 3):
        tasks["s", n] = lambda n=n: stat_send(n, stat_sum(n - 1))
    tasks["s", "z"] = stat_relay
    tasks["s", 4] = last_stats

    for task in ORDER:
        tasks[task]()
    all_sent(
        {
            "text": text,
            "image": image,
            "label": labels.at[0],
            "labels": labels,
            "sum": coded_out,
            "stat": stat_slots,
        }
    )


def on_device(picture, caption, labels, warmth, offset):
    vmem = pl.BlockSpec(memory_space=pltpu.VMEM)
    smem = pl.BlockSpec(memory_space=pltpu.SMEM)
    hbm = pl.BlockSpec(memory_space=pl.ANY)
    grad = pltpu.VMEM((ROWS, D), jnp.float32)
    sums = jax.ShapeDtypeStruct((3,), jnp.float32)
    return pl.pallas_call(
        kernel,
        out_shape=(grad, grad, sums),
        in_specs=[hbm, hbm, vmem, hbm, hbm],
        out_specs=(vmem, vmem, smem),
        scratch_shapes=[
            pltpu.VMEM((TILE, D), jnp.bfloat16),
            pltpu.VMEM((TILE, D), jnp.bfloat16),
            pltpu.VMEM((2, NZ, 8, LANES), jnp.int32),
            pltpu.VMEM((8, TILE), jnp.int32),
            pltpu.VMEM((2, 256, 512), jnp.float32),
            pltpu.VMEM((TILE, TILE), jnp.bfloat16),
            pltpu.VMEM((TILE, D), jnp.float32),
            pltpu.VMEM((TILE, D), jnp.float32),
            pltpu.VMEM((TILE // HALF, QUARTER, LANES), jnp.float32),
            pltpu.VMEM((TILE // HALF, QUARTER, LANES), jnp.float32),
            pltpu.VMEM((N_TILES, QUARTER, LANES), jnp.int16),
            pltpu.VMEM((N_TILES, QUARTER, LANES), jnp.int16),
            pltpu.VMEM((3, 8, LANES), jnp.float32),
            pltpu.VMEM((2 + NX + NY + NZ, 8, LANES), jnp.float32),
            pltpu.SMEM((1,), jnp.float32),
            pltpu.SMEM((1,), jnp.float32),
            pltpu.SemaphoreType.DMA((4,)),
            pltpu.SemaphoreType.DMA((N_SEND,)),
            pltpu.SemaphoreType.DMA((N_RECV,)),
        ],
        compiler_params=pltpu.CompilerParams(
            collective_id=0, has_side_effects=True, vmem_limit_bytes=56 << 20
        ),
    )(warmth, offset, labels.reshape(4, LANES), picture, caption)


def solution(mesh):
    rows = P(("grp", "mem"), None)
    return jax.shard_map(
        on_device,
        mesh=mesh,
        in_specs=(rows, rows, P("grp"), P(), P()),
        out_specs=(rows, rows, P()),
        check_vma=False,
    )
```

```python
import jax
import jax.numpy as jnp
from jax import lax
from jax.experimental import pallas as pl
from jax.experimental.pallas import tpu as pltpu
from jax.sharding import PartitionSpec as P

MESH = pl.DeviceIdType.MESH
NX, NY, NZ = 4, 4, 8
ROWS = 64
HALF, QUARTER = 32, 16
D = 1152
LANES = 128
WIDE = D // LANES
TILE = 1024
PAIRS = 16384
LEVELS = 32000.0
SMALLEST = 1e-30

FAR_FIRST = (2, 1, 3, 0)
TEXT_HALVES = [
    (h, i, j)
    for i in FAR_FIRST
    for h in (0, 1)
    for j in (FAR_FIRST if h == 0 else FAR_FIRST[::-1])
]
TEXT_AT = {key: n * HALF for n, key in enumerate(TEXT_HALVES)}
PARTS = ((4, 3), (5, 2), (6, 1), (7, 0))
IMAGE_ORDER = [(c, d) for part in PARTS for c in (1, 0) for d in part]
IMAGE_AT = {key: n * ROWS for n, key in enumerate(IMAGE_ORDER)}
N_SEND, N_RECV = 6, 128
N_TILES = 1152
ORDER = [
    "begin", ("z", 7, 0), ("z", 1, 48), ("t", 0, 1, 0), ("t", 1, 3, 0), ("z", 1, 32), ("t", 1, 1, 0),
    ("z", 7, 16), ("z", 1, 16), ("t", 0, 3, 0), ("z", 7, 32), ("z", 7, 48), ("z", 1, 0), ("t", 1, 2, 0),
    ("t", 0, 2, 0), "label", ("t", 1, 0, 3), ("z", 6, 0), ("z", 2, 48), ("t", 1, 0, 1), ("z", 6, 16),
    ("t", 1, 3, 3), ("z", 2, 32), ("t", 0, 0, 3), ("c", 3), ("t", 0, 0, 1), ("t", 0, 1, 3), ("z", 6, 32),
    ("t", 1, 1, 3), ("z", 2, 16), ("t", 0, 1, 1), ("t", 1, 3, 1), ("z", 6, 48), ("z", 2, 0), ("t", 0, 3, 3),
    ("z", 5, 0), ("t", 1, 1, 1), ("t", 0, 3, 1), ("z", 3, 48), ("t", 1, 2, 1), "far", ("t", 0, 2, 1),
    ("z", 5, 16), ("c", 2), ("t", 0, 2, 3), ("z", 3, 32), ("t", 1, 2, 3), ("t", 1, 2, 2), ("t", 0, 2, 2),
    ("t", 0, 0, 2), ("t", 1, 0, 2), "labels", ("p", 0, 1), ("p", 3, 1), ("t", 1, 3, 2), ("t", 0, 1, 2),
    ("z", 3, 16), ("z", 5, 32), ("z", 5, 48), ("t", 0, 3, 2), ("z", 3, 0), ("p", 2, 1), ("z", 4, 0),
    ("z", 4, 16), ("z", 4, 48), ("z", 4, 32), ("t", 1, 1, 2), ("c", 1), ("p", 1, 1), ("T", 1, "a"), ("c", 0),
    ("p", 1, 0), ("p", 3, 0), ("p", 2, 0), ("p", 0, 0), ("s", 0), ("T", 0, "b"), ("I", 0, "b"), ("co", 0),
    ("T", 2, "a"), ("I", 1, "b"), ("cw", 4), ("sf", 2), ("zs", 4, 0), ("zs", 4, 16), ("co", 1), ("I", 2, "a"),
    ("cw", 3), ("s", 1), ("T", 1, "b"), ("cw", 5), ("zs", 3, 32), ("zs", 3, 48), ("sf", 1), ("T", 2, "b"),
    ("sf", 3), ("zs", 3, 0), ("sn", 2), ("I", 2, "b"), ("s", 2), ("co", 2), ("zs", 3, 16), ("I", 3, "a"),
    ("cw", 2), ("sn", 1), ("cw", 6), ("zs", 2, 32), ("zs", 2, 48), ("sn", 3), ("I", 3, "b"), ("co", 3),
    ("zs", 2, 0), ("f", 2), ("s", 3), ("zs", 2, 16), ("T", 3, "a"), ("T", 3, "b"), ("sf", 0), ("sn", 0),
    ("cw", 0), ("cw", 7), ("cw", 1), ("zs", 1, 48), ("zs", 1, 0), ("f", 1), ("zs", 1, 32), ("f", 3),
    ("s", "z"), ("zs", 1, 16), ("zl", 0), ("zl", 48), ("tl", 0), ("s", 4), ("zl", 32), ("zl", 16), ("tl", 1),
]


def fold(values):
    rows, columns = values.shape
    parts = [
        values[r : r + 8, c : c + LANES]
        for r in range(0, rows, 8)
        for c in range(0, columns, LANES)
    ]
    while len(parts) > 1:
        parts = [a + b for a, b in zip(parts[::2], parts[1::2], strict=True)]
    return parts[0]


def kernel(
    warmth_hbm,
    offset_hbm,
    labels_ref,
    image_hbm,
    text_hbm,
    image_out,
    text_out,
    stats_out,
    image,
    text,
    labels,
    label_row,
    scores,
    coef,
    image_sum,
    text_sum,
    image_top,
    text_top,
    coded_out,
    coded_in,
    stats,
    stat_slots,
    warmth_ref,
    offset_ref,
    local_sem,
    send_sem,
    recv_sem,
):
    group, member = lax.axis_index("grp"), lax.axis_index("mem")
    core, x, z_high = lax.rem(group, 2), lax.rem(group // 2, NX), group // (2 * NX)
    y, z_low = lax.rem(member, NY), member // NY
    z = z_high * 2 + z_low

    def device(dx=0, dy=0, dz=0, dc=0):
        to_x, to_y = lax.rem(x + dx + NX, NX), lax.rem(y + dy + NY, NY)
        to_z, to_c = lax.rem(z + dz + NZ, NZ), lax.rem(core + dc, 2)
        return ((to_z // 2 * NX + to_x) * 2 + to_c, lax.rem(to_z, 2) * NY + to_y)

    ahead = {"x": device(dx=1), "y": device(dy=1), "z": device(dz=1)}
    behind = {"x": device(dx=-1), "y": device(dy=-1), "z": device(dz=-1)}
    beyond = {"x": device(dx=2), "y": device(dy=2)}
    other = device(dc=1)
    near_steps, relays = (1, -1, 2, -2), ((6, 1), (6, 2), (2, -1))

    own_image = pltpu.make_async_copy(
        image_hbm, image.at[pl.ds(IMAGE_AT[0, 0], ROWS)], local_sem.at[0]
    )
    own_text = pltpu.make_async_copy(
        text_hbm, text.at[pl.ds(TEXT_AT[0, 0, 0], ROWS)], local_sem.at[1]
    )
    scalars = [
        pltpu.make_async_copy(warmth_hbm, warmth_ref, local_sem.at[2]),
        pltpu.make_async_copy(offset_hbm, offset_ref, local_sem.at[3]),
    ]
    own_image.start()
    own_text.start()
    for copy in scalars:
        copy.start()

    partners = [other]
    partners += [device(dx=d) for d in range(1, NX)]
    partners += [device(dy=d) for d in range(1, NY)]
    partners += [device(dz=d) for d in near_steps]
    barrier = pltpu.get_barrier_semaphore()
    for partner in partners:
        pl.semaphore_signal(barrier, inc=1, device_id=partner, device_id_type=MESH)
    pl.semaphore_wait(barrier, len(partners))

    recv_of, sent_of = {}, {}

    def place(key):
        return recv_sem.at[recv_of.setdefault(key, len(recv_of))]

    def send(kind, amount, source, target, to, key):
        at = list(sent_of).index(kind) if kind in sent_of else len(sent_of)
        sent_of[kind] = sent_of.get(kind, 0) + amount
        pltpu.make_async_remote_copy(
            src_ref=source,
            dst_ref=target,
            send_sem=send_sem.at[at],
            recv_sem=place(key),
            device_id=to,
            device_id_type=MESH,
        ).start()

    def expect(key, ref):
        pltpu.make_async_remote_copy(
            src_ref=ref,
            dst_ref=ref,
            send_sem=send_sem.at[0],
            recv_sem=place(key),
            device_id=other,
            device_id_type=MESH,
        ).wait_recv()

    def all_sent(refs):
        for at, (kind, amount) in enumerate(sent_of.items()):
            ref = refs[kind].at[pl.ds(0, amount)]
            pltpu.make_async_remote_copy(
                src_ref=ref,
                dst_ref=ref,
                send_sem=send_sem.at[at],
                recv_sem=recv_sem.at[0],
                device_id=other,
                device_id_type=MESH,
            ).wait_send()

    def axis_of(h, nth):
        return "xy"[(h + nth) % 2]

    tasks = {}

    def send_text(h, i, j, row, rows, nth, step):
        there = (h, (i - step) % 4, j) if nth == 0 else (h, i, (j - step) % 4)
        send(
            "text",
            rows,
            text.at[pl.ds(TEXT_AT[h, i, j] + row, rows)],
            text.at[pl.ds(TEXT_AT[there] + row, rows)],
            {1: ahead, -1: behind, 2: beyond}[step][axis_of(h, nth)],
            ("text", *there),
        )

    def spread(h, i, j, nth):
        send_text(h, i, j, 0, HALF, nth, 1)
        send_text(h, i, j, 0, HALF, nth, -1)

    def on_text(h, i, j):
        expect(("text", h, i, j), text.at[pl.ds(0, HALF)])
        if j == 0:
            spread(h, i, j, 1)
            if i == 2:
                send_text(h, i, j, 0, HALF, 1, 2)
        elif j == 3 and i != 2:
            send_text(h, i, j, 0, QUARTER, 1, 1)
        elif j == 1 and i != 2:
            send_text(h, i, j, QUARTER, QUARTER, 1, -1)

    for h in (0, 1):
        for i in range(4):
            for j in range(4):
                if i or j:
                    tasks["t", h, i, j] = lambda a=(h, i, j): on_text(*a)

    def send_image(d, row, rows, to, there, key):
        send(
            "image",
            rows,
            image.at[pl.ds(IMAGE_AT[0, d] + row, rows)],
            image.at[pl.ds(IMAGE_AT[there] + row, rows)],
            to,
            key,
        )

    def across(d, row, rows):
        part = next(n for n, p in enumerate(PARTS) if d in p)
        send_image(d, row, rows, other, (1, d), ("across", part))

    def along_z(d, row, step):
        there = (d - step) % NZ
        to = (ahead if step == 1 else behind)["z"]
        send_image(d, row, QUARTER, to, (0, there), ("z", there, row))

    def on_image(d, row):
        expect(("z", d, row), image.at[pl.ds(0, QUARTER)])
        if d > 5 or (d == 5 and row < HALF):
            along_z(d, row, 1)
        if d < 3 or (d == 3 and row >= HALF):
            along_z(d, row, -1)
        if row % HALF == (QUARTER if d >= 4 and not (d == 4 and row >= HALF) else 0):
            across(d, row - row % HALF, HALF)

    for d in range(1, NZ):
        for row in range(0, ROWS, QUARTER):
            tasks["z", d, row] = lambda a=(d, row): on_image(*a)
    for n in range(len(PARTS)):
        tasks["c", n] = lambda n=n: expect(
            ("across", n), image.at[pl.ds(0, ROWS * 2)]
        )

    def begin():
        own_text.wait()
        for h in (0, 1):
            spread(h, 0, 0, 0)
        own_image.wait()
        for row in range(0, ROWS, QUARTER):
            along_z(0, row, 1)
            along_z(0, ROWS - QUARTER - row, -1)
        for h in (0, 1):
            send_text(h, 0, 0, 0, HALF, 0, 2)
        for h in (0, 1):
            spread(h, 0, 0, 1)
        across(0, 0, ROWS)
        mine = jnp.broadcast_to(labels_ref[pl.ds(member // 2, 1), :], (8, LANES))
        turned = pltpu.roll(mine, ROWS, 1)
        in_upper = jnp.broadcast_to(lax.rem(member, 2), (8, LANES)) == 1
        labels[0, 0] = jnp.where((lane >= ROWS) == in_upper, mine, turned)
        for d in near_steps:
            there = labels.at[0, -d % NZ]
            send("label", 1, labels.at[0, 0], there, device(dz=d), "label")
        for n in range(3):
            stats[n] = zero

    def on_label():
        expect("label", labels.at[0, pl.ds(0, len(near_steps))])
        for d, step in relays:
            here, there = labels.at[0, d], labels.at[0, (d - step) % NZ]
            send("label", 1, here, there, device(dz=step), "far")

    def on_far_label():
        expect("far", labels.at[0, pl.ds(0, len(relays))])
        here, there = labels.at[pl.ds(0, 1)], labels.at[pl.ds(1, 1)]
        send("labels", 1, here, there, other, "labels")

    def on_labels():
        expect("labels", labels.at[pl.ds(0, 1)])
        for at in range(0, TILE // ROWS, 2):
            label_row[:, at * ROWS : (at + 2) * ROWS] = jnp.where(
                lane < ROWS, labels[IMAGE_ORDER[at]], labels[IMAGE_ORDER[at + 1]]
            )

    for copy in scalars:
        copy.wait()
    lane = lax.broadcasted_iota(jnp.int32, (8, LANES), 1)
    zero = jnp.zeros((8, LANES), jnp.float32)
    warmth = jnp.exp(jnp.full((1, 1), warmth_ref[0], jnp.float32))
    offset = offset_ref[0]
    stretch = warmth * (1.0 / PAIRS)
    tasks["begin"] = begin
    tasks["label"] = on_label
    tasks["far"] = on_far_label
    tasks["labels"] = on_labels

    def pairs(chunk, side):
        first, left = chunk * 256, side * 512
        slot = (chunk + side) % 2
        scores[slot] = lax.dot_general(
            text[pl.ds(first, 256), :],
            image[pl.ds(left, 512), :],
            (((1,), (1,)), ((), ())),
            preferred_element_type=jnp.float32,
        )
        for row in range(0, 256, HALF):
            h, i, j = TEXT_HALVES[(first + row) // HALF]
            rx, ry = (i, j) if h == 0 else (j, i)
            owner_x, owner_y = lax.rem(x + rx, NX), lax.rem(y + ry, NY)
            base = (
                ((z_high * NX + owner_x) * 2 + core) * 8 + z_low * NY + owner_y
            ) * ROWS + h * HALF
            position = lax.broadcasted_iota(jnp.int32, (HALF, 1), 0) + base
            for column in (0, 256):
                s = scores[slot, pl.ds(row, HALF), pl.ds(column, 256)]
                logit = s * warmth + offset
                matched = label_row[0:1, pl.ds(left + column, 256)] == position
                signed = jnp.where(matched, -logit, logit)
                e = jnp.exp(-jnp.abs(signed))
                one_e = 1.0 + e
                inverse = 1.0 / one_e
                chance = jnp.where(signed >= 0, inverse, e * inverse)
                factor = jnp.where(matched, -chance, chance)
                coef[pl.ds(first + row, HALF), pl.ds(left + column, 256)] = factor.astype(
                    jnp.bfloat16
                )
                grown = zero
                for r in range(0, HALF, 8):
                    for c in range(0, 256, LANES):
                        piece = slice(r, r + 8), slice(c, c + LANES)
                        grown = grown * one_e[piece] + e[piece]
                stats[0] += fold(jnp.maximum(signed, 0.0)) + jnp.log1p(grown)
                stats[1] += fold(factor * s)
                stats[2] += fold(factor)

    def find_tops(sums, tops, first):
        for row in range(first, first + 256, HALF):
            top = None
            for r in range(0, HALF, 8):
                for c in range(0, D, LANES):
                    part = jnp.abs(sums[pl.ds(row + r, 8), c : c + LANES])
                    top = part if top is None else jnp.maximum(top, part)
            top = jnp.max(jnp.max(top, axis=1, keepdims=True), axis=0, keepdims=True)
            power = jnp.ceil(jnp.log2(jnp.maximum(top, SMALLEST)))
            tops[row // HALF] = jnp.broadcast_to(power, (QUARTER, LANES))

    def text_part(chunk, step):
        at = pl.ds(chunk * 256, 256)
        along = {"a": pl.ds(512, 512), "b": pl.ds(0, 512 if chunk else TILE)}[step]
        product = jnp.dot(
            coef[at, along], image[along, :], preferred_element_type=jnp.float32
        )
        if step == "b" and chunk:
            product = product + text_sum[at, :]
        text_sum[at, :] = product
        if step == "b":
            find_tops(text_sum, text_top, chunk * 256)

    def image_part(part, step):
        at = pl.ds(part * 256, 256)
        rest = part >= 2
        along = {"a": pl.ds(256, 768), "b": pl.ds(0, 256 if rest else TILE)}[step]
        product = lax.dot_general(
            coef[along, at],
            text[along, :],
            (((0,), (0,)), ((), ())),
            preferred_element_type=jnp.float32,
        )
        if step == "b" and rest:
            product = product + image_sum[at, :]
        image_sum[at, :] = product
        if step == "b":
            find_tops(image_sum, image_top, part * 256)

    messages = {}
    used = [0]

    def arrived(parts):
        found = {}
        for adds in parts:
            for name, _ in adds:
                if name not in found:
                    power = coded_in[messages[name]].astype(jnp.float32)
                    found[name] = jnp.exp2(power) * (1.0 / LEVELS), power
        return found

    def summed(sums, row, wide, adds, found):
        value = sums[pl.ds(row, QUARTER), wide * LANES : (wide + 1) * LANES]
        for name, nth in adds:
            tile = coded_in[messages[name] + 1 + nth * WIDE + wide]
            value = value + tile.astype(jnp.float32) * found[name][0]
        return value

    def send_sums(*sending):
        ready = []
        for name, sums, tops, row, parts, to, key in sending:
            start, count = used[0], 1 + len(parts) * WIDE
            messages[name] = start
            used[0] += count
            found = arrived(parts)
            powers = [tops[row // HALF]]
            if len(parts) * QUARTER > HALF:
                powers[0] = jnp.maximum(powers[0], tops[row // HALF + 1])
            powers += [power for _, power in found.values()]
            while len(powers) > 1:
                powers = powers[2:] + [jnp.maximum(powers[0], powers[1]) + 1.0]
            coded_out[start] = powers[0].astype(jnp.int16)
            scale = jnp.exp2(-powers[0]) * LEVELS
            for n, adds in enumerate(parts):
                for wide in range(WIDE):
                    value = summed(sums, row + n * QUARTER, wide, adds, found)
                    coded_out[start + 1 + n * WIDE + wide] = (
                        jnp.round(value * scale).astype(jnp.int32).astype(jnp.int16)
                    )
            ready.append((pl.ds(start, count), count, to, key))
        for at, count, to, key in ready:
            send("sum", count, coded_out.at[at], coded_in.at[at], to, key)

    def await_sum(key, *sizes):
        count = sum(1 + rows // QUARTER * WIDE for rows in sizes)
        expect(key, coded_in.at[pl.ds(0, count)])

    def direct(i):
        return i == 0

    def second_far(i):
        sending = []
        for h in (0, 1):
            axis, at = axis_of(h, 1), TEXT_AT[h, i, 2]
            if direct(i):
                name, to = (h, i, "far"), beyond[axis]
                sending.append(
                    (name, text_sum, text_top, at, [[], []], to, (h, i, "n"))
                )
                continue
            for far, row, to in (("fa", 0, ahead), ("fb", QUARTER, behind)):
                name = (h, i, far)
                sending.append(
                    (name, text_sum, text_top, at + row, [[]], to[axis], name)
                )
        send_sums(*sending)

    def second_near(i):
        sending = []
        for h in (0, 1):
            for j, far, near, to in ((1, "fa", "na", ahead), (3, "fb", "nb", behind)):
                parts = [[], []]
                if not direct(i):
                    await_sum((h, i, far), QUARTER)
                    parts[j == 3].append(((h, i, far), 0))
                at, to = TEXT_AT[h, i, j], to[axis_of(h, 1)]
                name = (h, i, near)
                sending.append((name, text_sum, text_top, at, parts, to, (h, i, "n")))
        send_sums(*sending)

    def line(h, i, nth):
        adds = [((h, i, "na"), nth), ((h, i, "nb"), nth)]
        return adds + [((h, i, "far"), nth)] if direct(i) else adds

    def first(i):
        sending = []
        for h in (0, 1):
            await_sum((h, i, "n"), *[HALF] * (3 if direct(i) else 2))
            to = {1: ahead, 2: beyond, 3: behind}[i][axis_of(h, 0)]
            parts = [line(h, i, 0), line(h, i, 1)]
            at = TEXT_AT[h, i, 0]
            sending.append(((h, "n", i), text_sum, text_top, at, parts, to, (h, "n")))
        send_sums(*sending)

    def text_last(h):
        await_sum((h, 0, "n"), *[HALF] * (3 if direct(0) else 2))
        await_sum((h, "n"), HALF, HALF, HALF)
        for n in (0, 1):
            adds = line(h, 0, n) + [((h, "n", i), n) for i in (1, 2, 3)]
            found = arrived([adds])
            at = h * HALF + n * QUARTER
            row = TEXT_AT[h, 0, 0] + n * QUARTER
            for wide in range(WIDE):
                value = summed(text_sum, row, wide, adds, found)
                text_out[at : at + QUARTER, wide * LANES : (wide + 1) * LANES] = (
                    value * stretch
                )

    for i in range(4):
        tasks["sf", i] = lambda i=i: second_far(i)
        tasks["sn", i] = lambda i=i: second_near(i)
        if i:
            tasks["f", i] = lambda i=i: first(i)
    for h in (0, 1):
        tasks["tl", h] = lambda h=h: text_last(h)

    def to_other(n):
        sending = []
        for d in PARTS[n]:
            parts = [[] for _ in range(4)]
            at = IMAGE_AT[1, d]
            sending.append((("c", d), image_sum, image_top, at, parts, other, ("c", d)))
        send_sums(*sending)

    def z_adds(d, row):
        adds = [(("c", d), row // QUARTER)]
        if d < 4 and (d < 3 or row < HALF):
            adds.append((("za", d + 1, row), 0))
        if (d > 4 or d == 0) and (d != 5 or row >= HALF):
            adds.append((("zb", (d - 1) % NZ, row), 0))
        return adds

    def z_send(far, row):
        sending = []
        for d, r, way, to in (
            (far, row, "za", ahead),
            (NZ - far, ROWS - QUARTER - row, "zb", behind),
        ):
            adds = z_adds(d, r)
            for name, _ in adds[1:]:
                await_sum(name, QUARTER)
            name, at = (way, d, r), IMAGE_AT[0, d] + r
            sending.append((name, image_sum, image_top, at, [adds], to["z"], name))
        send_sums(*sending)

    def image_last(row):
        adds = z_adds(0, row)
        for name, _ in adds[1:]:
            await_sum(name, QUARTER)
        found = arrived([adds])
        for wide in range(WIDE):
            value = summed(image_sum, IMAGE_AT[0, 0] + row, wide, adds, found)
            image_out[row : row + QUARTER, wide * LANES : (wide + 1) * LANES] = (
                value * stretch
            )

    for n in range(4):
        tasks["co", n] = lambda n=n: to_other(n)
        for step in "ab":
            if step == "b" or n >= 1:
                tasks["T", n, step] = lambda a=(n, step): text_part(*a)
            if step == "b" or n >= 2:
                tasks["I", n, step] = lambda a=(n, step): image_part(*a)
        for chunk in range(4):
            if n < 2:
                tasks["p", chunk, n] = lambda a=(chunk, n): pairs(*a)
    for d in range(NZ):
        tasks["cw", d] = lambda d=d: await_sum(("c", d), ROWS)
        for row in range(0, ROWS, QUARTER):
            if d == 0:
                tasks["zl", row] = lambda row=row: image_last(row)
            elif d < 4 or (d == 4 and row < HALF):
                tasks["zs", d, row] = lambda a=(d, row): z_send(*a)

    stat_axes = (
        (2, core, lambda d: device(dc=d)),
        (NX, x, lambda d: device(dx=d)),
        (NY, y, lambda d: device(dy=d)),
        (NZ, z, lambda d: device(dz=d)),
    )

    def stat_send(nth, value):
        base = sum(a[0] for a in stat_axes[:nth])
        size, me, to = stat_axes[nth]
        stat_slots[base + me] = value
        for d in near_steps if size == NZ else range(1, size):
            slot = stat_slots.at[pl.ds(base + me, 1)]
            send("stat", 1, slot, slot, to(d), ("stat", nth))

    def stat_relay():
        base = 2 + NX + NY
        expect(("stat", 3), stat_slots.at[pl.ds(0, len(near_steps))])
        for d, step in relays:
            slot = stat_slots.at[pl.ds(base + lax.rem(z + d, NZ), 1)]
            send("stat", 1, slot, slot, device(dz=step), ("stat", 4))

    def stat_sum(nth):
        base, size = sum(a[0] for a in stat_axes[:nth]), stat_axes[nth][0]
        if size == NZ:
            expect(("stat", 4), stat_slots.at[pl.ds(0, len(relays))])
        else:
            expect(("stat", nth), stat_slots.at[pl.ds(0, size - 1)])
        value = stat_slots[base]
        for n in range(1, size):
            value = value + stat_slots[base + n]
        return value

    def first_stats():
        rows = [jnp.sum(stats[n], axis=0, keepdims=True) for n in range(3)]
        rows.append(jnp.zeros((5, LANES), jnp.float32))
        stat_send(0, jnp.concatenate(rows, axis=0))

    def last_stats():
        everyone = stat_sum(3)
        share = 1.0 / float(PAIRS * PAIRS)
        stats_out[0] = jnp.sum(everyone[0:1, :]) * share
        stats_out[1] = jnp.sum(everyone[1:2, :] * warmth) * share
        stats_out[2] = jnp.sum(everyone[2:3, :]) * share

    tasks["s", 0] = first_stats
    for n in (1, 2, 3):
        tasks["s", n] = lambda n=n: stat_send(n, stat_sum(n - 1))
    tasks["s", "z"] = stat_relay
    tasks["s", 4] = last_stats

    for task in ORDER:
        tasks[task]()
    all_sent(
        {
            "text": text,
            "image": image,
            "label": labels.at[0],
            "labels": labels,
            "sum": coded_out,
            "stat": stat_slots,
        }
    )


def on_device(picture, caption, labels, warmth, offset):
    vmem = pl.BlockSpec(memory_space=pltpu.VMEM)
    smem = pl.BlockSpec(memory_space=pltpu.SMEM)
    hbm = pl.BlockSpec(memory_space=pl.ANY)
    grad = pltpu.VMEM((ROWS, D), jnp.float32)
    sums = jax.ShapeDtypeStruct((3,), jnp.float32)
    return pl.pallas_call(
        kernel,
        out_shape=(grad, grad, sums),
        in_specs=[hbm, hbm, vmem, hbm, hbm],
        out_specs=(vmem, vmem, smem),
        scratch_shapes=[
            pltpu.VMEM((TILE, D), jnp.bfloat16),
            pltpu.VMEM((TILE, D), jnp.bfloat16),
            pltpu.VMEM((2, NZ, 8, LANES), jnp.int32),
            pltpu.VMEM((8, TILE), jnp.int32),
            pltpu.VMEM((2, 256, 512), jnp.float32),
            pltpu.VMEM((TILE, TILE), jnp.bfloat16),
            pltpu.VMEM((TILE, D), jnp.float32),
            pltpu.VMEM((TILE, D), jnp.float32),
            pltpu.VMEM((TILE // HALF, QUARTER, LANES), jnp.float32),
            pltpu.VMEM((TILE // HALF, QUARTER, LANES), jnp.float32),
            pltpu.VMEM((N_TILES, QUARTER, LANES), jnp.int16),
            pltpu.VMEM((N_TILES, QUARTER, LANES), jnp.int16),
            pltpu.VMEM((3, 8, LANES), jnp.float32),
            pltpu.VMEM((2 + NX + NY + NZ, 8, LANES), jnp.float32),
            pltpu.SMEM((1,), jnp.float32),
            pltpu.SMEM((1,), jnp.float32),
            pltpu.SemaphoreType.DMA((4,)),
            pltpu.SemaphoreType.DMA((N_SEND,)),
            pltpu.SemaphoreType.DMA((N_RECV,)),
        ],
        compiler_params=pltpu.CompilerParams(
            collective_id=0, has_side_effects=True, vmem_limit_bytes=56 << 20
        ),
    )(warmth, offset, labels.reshape(4, LANES), picture, caption)


def solution(mesh):
    rows = P(("grp", "mem"), None)
    return jax.shard_map(
        on_device,
        mesh=mesh,
        in_specs=(rows, rows, P("grp"), P(), P()),
        out_specs=(rows, rows, P()),
        check_vma=False,
    )
```
